512 devices in a mesh: day: 16 (over y, core), bl: 32 (over z, x).
Axes of the slice: x: 4, y: 8, z: 8, core: 2. Of those that a mesh axis runs over, the one named last changes fastest.
Arguments:
- visibility: bfloat16 [16, 16, 2, 2048, 512], P('day', None, None, 'bl'), may hold values from -6 to 6
- day_weight: float32 [16, 2048, 512], P('day', 'bl'), may hold values from 0.2 to 5
- day_offset: int32 [16], replicated, may hold values from 0 to 16, as said below
- pair_index: int32 [2048], replicated, may hold values from 0 to 3, as said below
- sep_index: int32 [2048], replicated, may hold values from 0 to 511, as said below
Outputs:
- skymap: float32 [512, 32, 4, 512], P('bl', 'day')
The draws below stay inside these ranges and needn't reach their ends.
Inputs may be any that keep to these rules, and one draw needn't show every extreme that they name: Each day's samples cover 32 bins day_offset to day_offset + 15; every 32 bin of the window is covered by some day; some day starts at 0 and some at 16. `pair_index`: each pair of cylinder separation and north-south separation is named by exactly one stacked baseline. `sep_index`: each pair of cylinder separation and north-south separation is named by exactly one stacked baseline.
All inputs are finite; a program needn't handle non-finite values.
Results may differ from the reference program's by a relative error of at most 0.0032.
Values may be sent and summed in bfloat16 or wider, within the bound.
No kernel may reach another device: no remote copies, remote signals or barrier semaphores. Data moves between devices by JAX's collectives and lax.ppermute only.
A program may use at most 64 MiB of HBM per device.

```python
import math
import jax
import jax.numpy as jnp
from jax import lax

FREQ = 512
PAIRS = 4
NSEP = 512
PIXELS = 512
BASES = 2048
DAYS = 16
RA = 32
SAMPLES = 16
DRIFT = 16
N_BL = 32


def shared_cells(key):
    return jax.random.permutation(key, PAIRS * NSEP).astype(jnp.int32)


def draw_day_offset(key, part):
    key = jax.random.fold_in(key, 11)
    first_key, second_key = jax.random.split(key)
    rank = jax.random.permutation(second_key, DAYS).astype(jnp.int32)
    step_up = -(-DRIFT // (DAYS - 1))
    spread = max(0, SAMPLES - step_up)
    base = rank * DRIFT // (DAYS - 1)
    jitter = jax.random.randint(first_key, (DAYS,), 0, spread + 1).astype(jnp.int32)
    jitter = jnp.where((rank == 0) | (rank == DAYS - 1), 0, jitter)
    offsets = jnp.clip(base - jitter, 0, DRIFT)
    return offsets.astype(jnp.int32)


def draw_pair_index(key, part):
    cells = shared_cells(key)
    return (cells // NSEP).astype(jnp.int32)


def draw_sep_index(key, part):
    cells = shared_cells(key)
    return (cells % NSEP).astype(jnp.int32)


def level_of(key, extent, cuts, low, high):
    level, own = 1.0, jax.random.fold_in(key, 6)
    for position, shards_of in cuts:
        steps = jnp.exp(jax.random.uniform(jax.random.fold_in(own, position), (shards_of,), jnp.float32, low / len(cuts), high / len(cuts)))
        level = level * jnp.repeat(steps, extent[position] // shards_of).reshape([-1 if axis == position else 1 for axis in range(len(extent))])
    return level


def bell_draw(stream_key, extent, scale, bound, cuts=(), dtype=jnp.bfloat16):
    values = scale * jax.random.normal(stream_key, extent, jnp.float32)
    if cuts:
        values = values * level_of(stream_key, extent, cuts, -0.22, 0.18)
    return jnp.clip(values, -bound, bound).astype(dtype)


def setup_inputs(seed: int = 0) -> dict:
    key_of = jax.random.split(jax.random.key(seed), 6)
    return {
        "visibility": bell_draw(key_of[0], (DAYS, SAMPLES, 2, BASES, FREQ), 1.0, 6.0, ((0, 16), (3, 32))),
        "day_weight": jnp.clip(jnp.exp(math.log(5.0) - 3.218876 * jax.random.uniform(key_of[1], (DAYS, BASES, FREQ), jnp.float32) ** level_of(key_of[1], (DAYS, BASES, FREQ), ((0, 16), (1, 32)), -0.2, 0.2)), 0.2, 5.0),
        "day_offset": draw_day_offset(jax.random.fold_in(key_of[5], 71), 0),
        "pair_index": draw_pair_index(jax.random.fold_in(key_of[5], 71), 0),
        "sep_index": draw_sep_index(jax.random.fold_in(key_of[5], 71), 0),
    }


phase_scale = 2.0 * 3.141592653589793 * 0.3048 / 299.792458


def ns_table(freq_at):
    freq_value = 800.0 - 400.0 * (freq_at + 0.5) / FREQ
    sine_dir = -1.0 + 2.0 * (jnp.arange(PIXELS).astype(jnp.float32) + 0.5) / PIXELS
    separation = jnp.arange(NSEP).astype(jnp.float32) - (NSEP // 2)
    factor = phase_scale * freq_value
    phase = factor[:, None, None] * separation[None, :, None] * sine_dir[None, None, :]
    return jnp.concatenate([jnp.cos(phase).astype(jnp.bfloat16), (-jnp.sin(phase)).astype(jnp.bfloat16)], axis=1)


def reference(visibility, day_weight, day_offset, pair_index, sep_index):
    ra_rows = jnp.arange(RA).astype(jnp.int32)
    shifted = ra_rows[None, :] - day_offset[:, None]
    valid = ((shifted >= 0) & (shifted < SAMPLES)).astype(jnp.float32)
    cell_key = (pair_index * NSEP + sep_index).astype(jnp.int32)
    block_freq = FREQ // N_BL

    def beam_block(block_at):
        first = (block_at * block_freq).astype(jnp.int32)
        vis_piece = lax.dynamic_slice_in_dim(visibility, first, block_freq, 4)
        weight_piece = lax.dynamic_slice_in_dim(day_weight, first, block_freq, 2)
        total = jnp.einsum('dr,dbf->rbf', valid, weight_piece, precision=lax.Precision.HIGHEST)

        def add_day(day_at, running):
            one_day = lax.dynamic_index_in_dim(vis_piece, day_at, 0, keepdims=False)
            start = lax.dynamic_index_in_dim(day_offset, day_at, 0, keepdims=False).astype(jnp.int32)
            zero_at = jnp.zeros((), jnp.int32)
            placed = lax.dynamic_update_slice(jnp.zeros((RA, 2, BASES, block_freq), jnp.bfloat16), one_day, (start, zero_at, zero_at, zero_at))
            weight_now = lax.dynamic_index_in_dim(weight_piece, day_at, 0, keepdims=False)
            return running + placed.astype(jnp.float32) * weight_now[None, None]

        summed = lax.fori_loop(0, DAYS, add_day, jnp.zeros((RA, 2, BASES, block_freq), jnp.float32))
        stack = (summed / total[:, None]).astype(jnp.bfloat16)
        spread = jnp.zeros((RA, 2, PAIRS * NSEP, block_freq), jnp.float32).at[:, :, cell_key, :].add(stack.astype(jnp.float32))
        grid = spread.astype(jnp.bfloat16).reshape(RA, 2, PAIRS, NSEP, block_freq)
        grid = grid.transpose(4, 0, 2, 1, 3).reshape(block_freq, RA * PAIRS, 2 * NSEP).astype(jnp.float32)
        freq_at = (first + jnp.arange(block_freq).astype(jnp.int32)).astype(jnp.float32)
        table = ns_table(freq_at).astype(jnp.float32)
        result = jnp.einsum('fmq,fqp->fmp', grid, table)
        return result.reshape(block_freq, RA, PAIRS, PIXELS)

    sky_map = lax.map(beam_block, jnp.arange(N_BL).astype(jnp.int32))
    return sky_map.reshape(FREQ, RA, PAIRS, PIXELS)
```

```python
import jax
import jax.numpy as jnp
from jax import lax
from jax.experimental import pallas as pl
from jax.experimental.pallas import tpu as pltpu
from jax.sharding import PartitionSpec as P

FREQ = 512
PAIRS = 4
NSEP = 512
PIXELS = 512
HALF = PIXELS // 2
RA = 32
RA_DEV = 2
SAMPLES = 16
DAYS = 16
BASES = 2048
N_BL = 32
BASE_LOC = BASES // N_BL
BAND = FREQ // N_BL
COARSE = 32
FINE = NSEP // COARSE
CHIPS = 8
HELD = 8
SCALE = 128.0

F32 = jnp.float32
BF16 = jnp.bfloat16
F16 = jnp.float16
MIB = 1 << 20

phase_scale = 2.0 * 3.141592653589793 * 0.3048 / 299.792458


def bins_below(offset, core):
    return 2 * (offset >> 2) + jnp.clip((offset & 3) - 2 * core, 0, 2)


def select_kernel(offset_ref, vis_ref, out_ref, sems):
    day = lax.axis_index("day")
    other = 1 - (day & 1)
    offset = offset_ref[day]
    first = bins_below(offset, other)
    copies = []
    for k in range(HELD):
        owned = first + k
        sample = 4 * (owned >> 1) + 2 * other + (owned & 1) - offset
        copies.append(
            pltpu.make_async_copy(
                vis_ref.at[sample], out_ref.at[owned & (HELD - 1)], sems.at[k]
            )
        )
        copies[-1].start()
    for copy in copies:
        copy.wait()


def select(day_offset, visibility):
    return pl.pallas_call(
        select_kernel,
        in_specs=[pl.BlockSpec(memory_space=pltpu.SMEM), pl.BlockSpec(memory_space=pl.ANY)],
        out_specs=pl.BlockSpec(memory_space=pltpu.VMEM),
        out_shape=jax.ShapeDtypeStruct((HELD, 2, BASE_LOC, FREQ), BF16),
        scratch_shapes=[pltpu.SemaphoreType.DMA((HELD,))],
        compiler_params=pltpu.CompilerParams(vmem_limit_bytes=8 * MIB),
        name="select",
    )(day_offset, visibility[0])


def chip_kernel(offset_ref, vis_ref, weight_ref, other_vis_ref, other_weight_ref, out_ref):
    day = lax.axis_index("day")
    core = day & 1
    chip = day >> 1
    offset = offset_ref[day]
    first = bins_below(offset_ref[day ^ 1], core)
    weight = weight_ref[...] * SCALE
    other_weight = other_weight_ref[...] * SCALE

    def one_bin(at, _):
        owned = 2 * ((chip + (at >> 1)) & (CHIPS - 1)) + (at & 1)
        sample = 4 * (owned >> 1) + 2 * core + (owned & 1) - offset
        valid = jnp.logical_and(sample >= 0, sample < SAMPLES)
        held = jnp.logical_and(owned >= first, owned < first + HELD)
        sample = jnp.clip(sample, 0, SAMPLES - 1)
        own = weight * jnp.where(valid, 1.0, 0.0)
        other = other_weight * jnp.where(held, 1.0, 0.0)
        for x in range(2):
            out_ref[at, x] = (
                vis_ref[sample, x].astype(F32) * own
                + other_vis_ref[owned & (HELD - 1), x].astype(F32) * other
            )
        return 0

    lax.fori_loop(0, 2 * CHIPS, one_bin, 0)


def chip_sums(day_offset, visibility, day_weight, other_vis, other_weight):
    rows = 16
    weight_spec = pl.BlockSpec((rows, FREQ), lambda i: (i, 0))
    return pl.pallas_call(
        chip_kernel,
        grid=(BASE_LOC // rows,),
        in_specs=[
            pl.BlockSpec(memory_space=pltpu.SMEM),
            pl.BlockSpec((SAMPLES, 2, rows, FREQ), lambda i: (0, 0, i, 0)),
            weight_spec,
            pl.BlockSpec((HELD, 2, rows, FREQ), lambda i: (0, 0, i, 0)),
            weight_spec,
        ],
        out_specs=pl.BlockSpec((2 * CHIPS, 2, rows, FREQ), lambda i: (0, 0, i, 0)),
        out_shape=jax.ShapeDtypeStruct((2 * CHIPS, 2, BASE_LOC, FREQ), F32),
        compiler_params=pltpu.CompilerParams(vmem_limit_bytes=16 * MIB),
        name="chip_sums",
    )(day_offset, visibility[0], day_weight[0], other_vis, other_weight)


def reduce_ring(chip_sum):
    up = [(2 * y + c, 2 * ((y + 1) % CHIPS) + c) for y in range(CHIPS) for c in range(2)]
    down = [(b, a) for a, b in up]
    streams = [[up, 0, 4, 1], [down, 1, 4, -1], [up, 1, 3, 1], [down, 0, 3, -1]]
    arrived = [None] * 4
    for step in range(4):
        for at, (pairs, which, hops, way) in enumerate(streams):
            if step >= hops:
                continue
            distance = (way * (hops - step)) % CHIPS
            own = chip_sum[2 * distance + which]
            if step:
                own = own + arrived[at].astype(F32)
            arrived[at] = lax.ppermute(own.astype(F16), "day", pairs)
    low = chip_sum[0] + arrived[0].astype(F32) + arrived[3].astype(F32)
    high = chip_sum[1] + arrived[1].astype(F32) + arrived[2].astype(F32)
    return low, high


def table_kernel(cos_a_ref, sin_a_ref, cos_b_ref, sin_b_ref, out_ref):
    cos_b = cos_b_ref[0]
    sin_b = sin_b_ref[0]
    for a in range(COARSE):
        cos_a = cos_a_ref[0, a : a + 1, :]
        sin_a = sin_a_ref[0, a : a + 1, :]
        rows = pl.ds(a * FINE, FINE)
        out_ref[0, rows, :HALF] = (cos_a * cos_b - sin_a * sin_b).astype(BF16)
        out_ref[0, rows, HALF:] = (-(sin_a * cos_b + cos_a * sin_b)).astype(BF16)


def ns_table():
    freq_at = (lax.axis_index("bl") * BAND + jnp.arange(BAND)).astype(F32)
    factor = phase_scale * (800.0 - 400.0 * (freq_at + 0.5) / FREQ)
    sine_dir = -1.0 + 2.0 * (jnp.arange(HALF).astype(F32) + 0.5) / PIXELS
    coarse = (jnp.arange(COARSE) * FINE - NSEP // 2).astype(F32)
    fine = jnp.arange(FINE).astype(F32)
    phase_a = factor[:, None, None] * coarse[None, :, None] * sine_dir[None, None, :]
    phase_b = factor[:, None, None] * fine[None, :, None] * sine_dir[None, None, :]
    spec_a = pl.BlockSpec((1, COARSE, HALF), lambda f: (f, 0, 0))
    spec_b = pl.BlockSpec((1, FINE, HALF), lambda f: (f, 0, 0))
    return pl.pallas_call(
        table_kernel,
        grid=(BAND,),
        in_specs=[spec_a, spec_a, spec_b, spec_b],
        out_specs=pl.BlockSpec((1, NSEP, 2 * HALF), lambda f: (f, 0, 0)),
        out_shape=jax.ShapeDtypeStruct((BAND, NSEP, 2 * HALF), BF16),
        compiler_params=pltpu.CompilerParams(vmem_limit_bytes=16 * MIB),
        cost_estimate=pl.CostEstimate(
            flops=6 * BAND * NSEP * HALF, bytes_accessed=4 * BAND * NSEP * HALF, transcendentals=0
        ),
        name="table",
    )(jnp.cos(phase_a), jnp.sin(phase_a), jnp.cos(phase_b), jnp.sin(phase_b))


def inverse_total(day_offset, all_weights):
    bins = lax.axis_index("day") * RA_DEV + jnp.arange(RA_DEV)
    sample = bins[:, None] - day_offset[None, :]
    valid = jnp.logical_and(sample >= 0, sample < SAMPLES).astype(F32)
    total = jnp.sum(valid[:, :, None, None] * all_weights[None].astype(F32), axis=1)
    return (1.0 / SCALE) / total


def pack_blocks(pieces, out_ref, rows):
    lane_group = lax.broadcasted_iota(jnp.int32, (8, 128), 1) // BAND
    for tile in range(FREQ // 128):
        parts = [piece[:, tile * 128 : (tile + 1) * 128] for piece in pieces]
        for step in (4, 2, 1):
            keep = (lane_group & step) == 0
            mixed = list(parts)
            for low in range(8):
                if low & step:
                    continue
                high = low | step
                mixed[low] = jnp.where(keep, parts[low], pltpu.roll(parts[high], step * BAND, 1))
                mixed[high] = jnp.where(
                    keep, pltpu.roll(parts[low], 128 - step * BAND, 1), parts[high]
                )
            parts = mixed
        for group in range(8):
            out_ref[tile * 8 + group, rows, :] = parts[group].astype(BF16)


def pack_kernel(low_ref, high_ref, inverse_ref, out_ref):
    half = BASE_LOC // 2
    for first in range(0, half, 16):
        for sub in range(0, 16, 8):
            rows = pl.ds(first + sub, 8)
            pieces = []
            for x in range(2):
                for r in range(RA_DEV):
                    for hi in range(2):
                        rows_in = pl.ds(hi * half + first + sub, 8)
                        pieces.append(
                            (low_ref, high_ref)[r][x, rows_in, :] * inverse_ref[r, rows_in, :]
                        )
            pack_blocks(pieces, out_ref, rows)


def pack(low, high, inverse):
    vmem = pl.BlockSpec(memory_space=pltpu.VMEM)
    return pl.pallas_call(
        pack_kernel,
        in_specs=[vmem, vmem, vmem],
        out_specs=vmem,
        out_shape=jax.ShapeDtypeStruct((N_BL, BASE_LOC // 2, 128), BF16),
        compiler_params=pltpu.CompilerParams(vmem_limit_bytes=16 * MIB),
        name="pack",
    )(low, high, inverse)


def beam_kernel(block_ref, pair_ref, sep_ref, table_ref, out_ref, grid_ref):
    flat = BASES // 2
    rows = RA_DEV * PAIRS

    @pl.when(pl.program_id(0) == 0)
    def _():
        turned = block_ref[...].astype(F32).reshape(flat, 128).T
        total = jnp.zeros((2 * rows * BAND, NSEP), F32)
        for hi in range(2):
            picked = [
                turned[(group * 2 + hi) * BAND : (group * 2 + hi + 1) * BAND] for group in range(4)
            ]
            pair = pair_ref[hi : hi + 1, :]
            masked = jnp.concatenate(
                [jnp.where(pair == c, part, 0.0) for part in picked for c in range(PAIRS)], axis=0
            ).astype(BF16)
            sep = sep_ref[:, hi : hi + 1]
            onehot = jnp.where(
                sep == lax.broadcasted_iota(jnp.int32, (flat, NSEP), 1), 1.0, 0.0
            ).astype(BF16)
            total = total + jnp.dot(masked, onehot, preferred_element_type=F32)
        for tile in range(NSEP // 128):
            grid_ref[tile] = total[:, tile * 128 : (tile + 1) * 128]

    flip = (
        lax.broadcasted_iota(jnp.int32, (HALF, HALF), 0)
        + lax.broadcasted_iota(jnp.int32, (HALF, HALF), 1)
        == HALF - 1
    )
    flip = jnp.where(flip, 1.0, 0.0).astype(BF16)
    count = table_ref.shape[0]
    odd_part = []
    for f in range(count):
        f_at = pl.program_id(0) * count + f
        cells = jnp.concatenate(
            [
                grid_ref[tile, pl.ds(f_at, 2 * rows, stride=BAND), :]
                for tile in range(NSEP // 128)
            ],
            axis=1,
        ).astype(BF16)
        even = jnp.dot(cells, table_ref[f], preferred_element_type=F32)
        cos_part = even[:rows, :HALF]
        sin_part = even[rows:, HALF:]
        out_ref[f, :, :HALF] = cos_part + sin_part
        odd_part.append(cos_part - sin_part)
    rest = jnp.concatenate(odd_part, axis=0)
    turned = jnp.zeros(rest.shape, F32)
    for _ in range(3):
        piece = rest.astype(BF16)
        rest = rest - piece.astype(F32)
        turned = turned + jnp.dot(piece, flip, preferred_element_type=F32)
    for f in range(count):
        out_ref[f, :, HALF:] = turned[f * rows : (f + 1) * rows]


def beam(block, pair_index, sep_index, table):
    flat = BASES // 2
    count = 4
    pair = pair_index.reshape(N_BL, 2, BASE_LOC // 2).transpose(1, 0, 2).reshape(2, flat)
    sep = sep_index.reshape(N_BL, 2, BASE_LOC // 2).transpose(0, 2, 1).reshape(flat, 2)
    whole = lambda shape: pl.BlockSpec(shape, lambda i: (0,) * len(shape))
    return pl.pallas_call(
        beam_kernel,
        grid=(BAND // count,),
        in_specs=[
            whole((N_BL, BASE_LOC // 2, 128)),
            whole((2, flat)),
            whole((flat, 2)),
            pl.BlockSpec((count, NSEP, 2 * HALF), lambda i: (i, 0, 0)),
        ],
        out_specs=pl.BlockSpec((count, RA_DEV * PAIRS, PIXELS), lambda i: (i, 0, 0)),
        out_shape=jax.ShapeDtypeStruct((BAND, RA_DEV * PAIRS, PIXELS), F32),
        scratch_shapes=[pltpu.VMEM((NSEP // 128, 2 * RA_DEV * PAIRS * BAND, 128), F32)],
        compiler_params=pltpu.CompilerParams(vmem_limit_bytes=32 * MIB),
        name="beam",
    )(block, pair, sep, table)


def day_stage(visibility, day_weight, day_offset):
    swap = [(d, d ^ 1) for d in range(DAYS)]
    other_vis = lax.ppermute(select(day_offset, visibility), "day", swap)
    other_weight = lax.ppermute(day_weight[0], "day", swap)
    all_weights = lax.all_gather(day_weight.astype(F16), "day", axis=0, tiled=True)
    low, high = reduce_ring(
        chip_sums(day_offset, visibility, day_weight, other_vis, other_weight)
    )
    return low, high, inverse_total(day_offset, all_weights)


def beam_stage(low, high, inverse, pair_index, sep_index):
    table = ns_table()
    packed = pack(low, high, inverse)
    block = lax.all_to_all(packed, "bl", split_axis=0, concat_axis=0, tiled=True)
    return beam(block, pair_index, sep_index, table)


def local(visibility, day_weight, day_offset, pair_index, sep_index):
    low, high, inverse = day_stage(visibility, day_weight, day_offset)
    result = beam_stage(low, high, inverse, pair_index, sep_index)
    return result.reshape(BAND, RA_DEV, PAIRS, PIXELS)


def solution(mesh):
    return jax.shard_map(
        local,
        mesh=mesh,
        in_specs=(P("day", None, None, "bl", None), P("day", "bl", None), P(), P(), P()),
        out_specs=P("bl", "day", None, None),
        check_vma=False,
    )
```

```python
import jax
import jax.numpy as jnp
from jax import lax
from jax.experimental import pallas as pl
from jax.experimental.pallas import tpu as pltpu
from jax.sharding import PartitionSpec as P

FREQ = 512
PAIRS = 4
NSEP = 512
PIXELS = 512
HALF = PIXELS // 2
RA = 32
RA_DEV = 2
SAMPLES = 16
DAYS = 16
BASES = 2048
N_BL = 32
BASE_LOC = BASES // N_BL
BAND = FREQ // N_BL
COARSE = 32
FINE = NSEP // COARSE
CHIPS = 8
HELD = 8
SCALE = 128.0
N_Z = 8
N_X = 4
SWAP = [(d, d ^ 1) for d in range(DAYS)]

F32 = jnp.float32
BF16 = jnp.bfloat16
F16 = jnp.float16
MIB = 1 << 20

phase_scale = 2.0 * 3.141592653589793 * 0.3048 / 299.792458


def bins_below(offset, core):
    return 2 * (offset >> 2) + jnp.clip((offset & 3) - 2 * core, 0, 2)


def select_kernel(offset_ref, weight_ref, vis_ref, out_ref, sems):
    day = lax.axis_index("day")
    other = 1 - (day & 1)
    offset = offset_ref[day]
    first = bins_below(offset, other)
    copies = []
    for k in range(HELD):
        owned = first + k
        sample = 4 * (owned >> 1) + 2 * other + (owned & 1) - offset
        copies.append(
            pltpu.make_async_copy(
                vis_ref.at[sample], out_ref.at[owned & (HELD - 1)], sems.at[k]
            )
        )
        copies[-1].start()
    weight = weight_ref[...]
    high = weight.astype(BF16)
    out_ref[HELD, 0] = high
    out_ref[HELD, 1] = (weight - high.astype(F32)).astype(BF16)
    for copy in copies:
        copy.wait()


def select(day_offset, day_weight, visibility):
    return pl.pallas_call(
        select_kernel,
        in_specs=[
            pl.BlockSpec(memory_space=pltpu.SMEM),
            pl.BlockSpec(memory_space=pltpu.VMEM),
            pl.BlockSpec(memory_space=pltpu.HBM),
        ],
        out_specs=pl.BlockSpec(memory_space=pltpu.VMEM),
        out_shape=jax.ShapeDtypeStruct((HELD + 1, 2, BASE_LOC, FREQ), BF16),
        scratch_shapes=[pltpu.SemaphoreType.DMA((HELD,))],
        compiler_params=pltpu.CompilerParams(vmem_limit_bytes=8 * MIB),
        name="select",
    )(day_offset, day_weight, visibility)


SENDS = (
    ((3, 0), (3, 1), (1, 0), (1, 1)),
    ((5, 0), (5, 1), (7, 0), (7, 1)),
    ((4, 0),),
    ((4, 1),),
    ((2, 0), (2, 1)),
    ((6, 0), (6, 1)),
    ((0, 0), (0, 1)),
)


def chip_kernel(offset_ref, vis_ref, weight_ref, other_ref, *out_refs):
    day = lax.axis_index("day")
    core = day & 1
    chip = day >> 1
    offset = offset_ref[day]
    first = bins_below(offset_ref[day ^ 1], core)
    weight = weight_ref[...] * SCALE
    other_weight = (other_ref[HELD, 0].astype(F32) + other_ref[HELD, 1].astype(F32)) * SCALE
    for out_ref, bins in zip(out_refs, SENDS):
        for at, (distance, which) in enumerate(bins):
            owned = 2 * ((chip + distance) & (CHIPS - 1)) + which
            sample = 4 * (owned >> 1) + 2 * core + which - offset
            valid = jnp.logical_and(sample >= 0, sample < SAMPLES)
            held = jnp.logical_and(owned >= first, owned < first + HELD)
            sample = jnp.clip(sample, 0, SAMPLES - 1)
            own = weight * jnp.where(valid, 1.0, 0.0)
            other = other_weight * jnp.where(held, 1.0, 0.0)
            for x in range(2):
                out_ref[at, x] = (
                    vis_ref[sample, x].astype(F32) * own
                    + other_ref[owned & (HELD - 1), x].astype(F32) * other
                )


def chip_sums(day_offset, visibility, day_weight, other):
    rows = 16
    block = lambda count: pl.BlockSpec((count, 2, rows, FREQ), lambda i: (0, 0, i, 0))
    return pl.pallas_call(
        chip_kernel,
        grid=(BASE_LOC // rows,),
        in_specs=[
            pl.BlockSpec(memory_space=pltpu.SMEM),
            block(SAMPLES),
            pl.BlockSpec((rows, FREQ), lambda i: (i, 0)),
            block(HELD + 1),
        ],
        out_specs=[block(len(bins)) for bins in SENDS],
        out_shape=[
            jax.ShapeDtypeStruct((len(bins), 2, BASE_LOC, FREQ), F32) for bins in SENDS
        ],
        compiler_params=pltpu.CompilerParams(vmem_limit_bytes=16 * MIB),
        name="chip_sums",
    )(day_offset, visibility, day_weight, other)


def reduce_ring(sums):
    def send(values, distance):
        pairs = [
            (2 * y + c, 2 * ((y + distance) % CHIPS) + c) for y in range(CHIPS) for c in range(2)
        ]
        return lax.ppermute(values.astype(F16), "day", pairs)

    near_up, near_down = send(sums[0], 1), send(sums[1], -1)
    far_up, far_down = send(sums[2], 2), send(sums[3], -2)
    middle_up = sums[4] + near_up[:2].astype(F32)
    middle_up = middle_up + jnp.pad(far_up.astype(F32), ((0, 1), (0, 0), (0, 0), (0, 0)))
    middle_down = sums[5] + near_down[:2].astype(F32)
    middle_down = middle_down + jnp.pad(far_down.astype(F32), ((1, 0), (0, 0), (0, 0), (0, 0)))
    last_up, last_down = send(middle_up, 2), send(middle_down, -2)
    return (
        sums[6]
        + near_up[2:].astype(F32)
        + near_down[2:].astype(F32)
        + last_up.astype(F32)
        + last_down.astype(F32)
    )


def table_kernel(cos_a_ref, sin_a_ref, cos_b_ref, sin_b_ref, out_ref):
    cos_b = cos_b_ref[0]
    sin_b = sin_b_ref[0]
    for a in range(COARSE):
        cos_a = cos_a_ref[0, a : a + 1, :]
        sin_a = sin_a_ref[0, a : a + 1, :]
        rows = pl.ds(a * FINE, FINE)
        out_ref[0, rows, :HALF] = (cos_a * cos_b - sin_a * sin_b).astype(BF16)
        out_ref[0, rows, HALF:] = (-(sin_a * cos_b + cos_a * sin_b)).astype(BF16)


def ns_table():
    freq_at = (lax.axis_index("bl") * BAND + jnp.arange(BAND)).astype(F32)
    factor = phase_scale * (800.0 - 400.0 * (freq_at + 0.5) / FREQ)
    sine_dir = -1.0 + 2.0 * (jnp.arange(HALF).astype(F32) + 0.5) / PIXELS
    coarse = (jnp.arange(COARSE) * FINE - NSEP // 2).astype(F32)
    fine = jnp.arange(FINE).astype(F32)
    phase_a = factor[:, None, None] * coarse[None, :, None] * sine_dir[None, None, :]
    phase_b = factor[:, None, None] * fine[None, :, None] * sine_dir[None, None, :]
    spec_a = pl.BlockSpec((1, COARSE, HALF), lambda f: (f, 0, 0))
    spec_b = pl.BlockSpec((1, FINE, HALF), lambda f: (f, 0, 0))
    return pl.pallas_call(
        table_kernel,
        grid=(BAND,),
        in_specs=[spec_a, spec_a, spec_b, spec_b],
        out_specs=pl.BlockSpec((1, NSEP, 2 * HALF), lambda f: (f, 0, 0)),
        out_shape=pltpu.HBM((BAND, NSEP, 2 * HALF), BF16),
        compiler_params=pltpu.CompilerParams(vmem_limit_bytes=16 * MIB),
        cost_estimate=pl.CostEstimate(
            flops=6 * BAND * NSEP * HALF, bytes_accessed=4 * BAND * NSEP * HALF, transcendentals=0
        ),
        name="table",
    )(jnp.cos(phase_a), jnp.sin(phase_a), jnp.cos(phase_b), jnp.sin(phase_b))


def inverse_total(day_offset, day_weight):
    day = lax.axis_index("day")
    core = day & 1
    same = [[2 * y + c for y in range(CHIPS)] for c in range(2)]
    weights = lax.all_gather(day_weight, "day", axis=0, axis_index_groups=same)
    offsets = jnp.where(core == 0, day_offset[0::2], day_offset[1::2])

    def partial_total(owner):
        sample = (owner * RA_DEV + jnp.arange(RA_DEV))[:, None] - offsets[None, :]
        valid = jnp.logical_and(sample >= 0, sample < SAMPLES).astype(F32)
        return jnp.sum(valid[:, :, None, None] * weights[None], axis=1)

    other = lax.ppermute(partial_total(day ^ 1), "day", SWAP)
    return (1.0 / SCALE) / (partial_total(day) + other)


def pack_blocks(pieces, out_ref, rows):
    lane_group = lax.broadcasted_iota(jnp.int32, (8, 128), 1) // BAND
    for tile in range(FREQ // 128):
        parts = [piece[:, tile * 128 : (tile + 1) * 128] for piece in pieces]
        for step in (4, 2, 1):
            keep = (lane_group & step) == 0
            mixed = list(parts)
            for low in range(8):
                if low & step:
                    continue
                high = low | step
                mixed[low] = jnp.where(keep, parts[low], pltpu.roll(parts[high], step * BAND, 1))
                mixed[high] = jnp.where(
                    keep, pltpu.roll(parts[low], 128 - step * BAND, 1), parts[high]
                )
            parts = mixed
        for group in range(8):
            out_ref[tile * 8 + group, rows, :] = parts[group].astype(BF16)


def pack_kernel(sum_ref, inverse_ref, table_ref, out_ref):
    half = BASE_LOC // 2
    for first in range(0, half, 16):
        for sub in range(0, 16, 8):
            rows = pl.ds(first + sub, 8)
            pieces = []
            for x in range(2):
                for r in range(RA_DEV):
                    for hi in range(2):
                        rows_in = pl.ds(hi * half + first + sub, 8)
                        pieces.append(
                            sum_ref[r, x, rows_in, :] * inverse_ref[r, rows_in, :]
                        )
            pack_blocks(pieces, out_ref, rows)


def pack(summed, inverse, table):
    vmem = pl.BlockSpec(memory_space=pltpu.VMEM)
    return pl.pallas_call(
        pack_kernel,
        in_specs=[vmem, vmem, pl.BlockSpec(memory_space=pltpu.HBM)],
        out_specs=vmem,
        out_shape=jax.ShapeDtypeStruct((N_BL, BASE_LOC // 2, 128), BF16),
        compiler_params=pltpu.CompilerParams(vmem_limit_bytes=16 * MIB),
        name="pack",
    )(summed, inverse, table)


def beam_kernel(block_ref, pair_ref, sep_ref, table_ref, out_ref, grid_ref):
    flat = BASES // 2
    rows = RA_DEV * PAIRS

    @pl.when(pl.program_id(0) == 0)
    def _():
        turned = block_ref[...].astype(F32).reshape(flat, 128).T
        total = jnp.zeros((2 * rows * BAND, NSEP), F32)
        for hi in range(2):
            picked = [
                turned[(group * 2 + hi) * BAND : (group * 2 + hi + 1) * BAND] for group in range(4)
            ]
            pair = pair_ref[hi : hi + 1, :]
            masked = jnp.concatenate(
                [jnp.where(pair == c, part, 0.0) for part in picked for c in range(PAIRS)], axis=0
            ).astype(BF16)
            sep = sep_ref[:, hi : hi + 1]
            onehot = jnp.where(
                sep == lax.broadcasted_iota(jnp.int32, (flat, NSEP), 1), 1.0, 0.0
            ).astype(BF16)
            total = total + jnp.dot(masked, onehot, preferred_element_type=F32)
        for tile in range(NSEP // 128):
            grid_ref[tile] = total[:, tile * 128 : (tile + 1) * 128]

    flip = (
        lax.broadcasted_iota(jnp.int32, (HALF, HALF), 0)
        + lax.broadcasted_iota(jnp.int32, (HALF, HALF), 1)
        == HALF - 1
    )
    flip = jnp.where(flip, 1.0, 0.0).astype(BF16)
    count = table_ref.shape[0]
    odd_part = []
    for f in range(count):
        f_at = pl.program_id(0) * count + f
        cells = jnp.concatenate(
            [
                grid_ref[tile, pl.ds(f_at, 2 * rows, stride=BAND), :]
                for tile in range(NSEP // 128)
            ],
            axis=1,
        ).astype(BF16)
        even = jnp.dot(cells, table_ref[f], preferred_element_type=F32)
        cos_part = even[:rows, :HALF]
        sin_part = even[rows:, HALF:]
        out_ref[f, :, :HALF] = cos_part + sin_part
        odd_part.append(cos_part - sin_part)
    rest = jnp.concatenate(odd_part, axis=0)
    turned = jnp.zeros(rest.shape, F32)
    for _ in range(3):
        piece = rest.astype(BF16)
        rest = rest - piece.astype(F32)
        turned = turned + jnp.dot(piece, flip, preferred_element_type=F32)
    for f in range(count):
        out_ref[f, :, HALF:] = turned[f * rows : (f + 1) * rows]


def beam(block, pair_index, sep_index, table):
    flat = BASES // 2
    count = 4
    pair = pair_index.reshape(N_BL, 2, BASE_LOC // 2).transpose(1, 0, 2).reshape(2, flat)
    sep = sep_index.reshape(N_BL, 2, BASE_LOC // 2).transpose(0, 2, 1).reshape(flat, 2)
    whole = lambda shape: pl.BlockSpec(shape, lambda i: (0,) * len(shape))
    return pl.pallas_call(
        beam_kernel,
        grid=(BAND // count,),
        in_specs=[
            whole((N_BL, BASE_LOC // 2, 128)),
            whole((2, flat)),
            whole((flat, 2)),
            pl.BlockSpec((count, NSEP, 2 * HALF), lambda i: (i, 0, 0)),
        ],
        out_specs=pl.BlockSpec((count, RA_DEV * PAIRS, PIXELS), lambda i: (i, 0, 0)),
        out_shape=jax.ShapeDtypeStruct((BAND, RA_DEV * PAIRS, PIXELS), F32),
        scratch_shapes=[pltpu.VMEM((NSEP // 128, 2 * RA_DEV * PAIRS * BAND, 128), F32)],
        compiler_params=pltpu.CompilerParams(vmem_limit_bytes=32 * MIB),
        name="beam",
    )(block, pair, sep, table)


def day_stage(visibility, day_weight, day_offset):
    visibility, day_weight = visibility[0], day_weight[0]
    inverse = inverse_total(day_offset, day_weight)
    other = lax.ppermute(select(day_offset, day_weight, visibility), "day", SWAP)
    summed = reduce_ring(chip_sums(day_offset, visibility, day_weight, other))
    return summed, inverse


def exchange(packed):
    blocks = packed.reshape(N_Z, N_X, BASE_LOC // 2, 128)
    along_z = [[z * N_X + x for z in range(N_Z)] for x in range(N_X)]
    along_x = [[z * N_X + x for x in range(N_X)] for z in range(N_Z)]
    blocks = lax.all_to_all(
        blocks, "bl", split_axis=0, concat_axis=0, axis_index_groups=along_z, tiled=True
    )
    blocks = lax.all_to_all(
        blocks, "bl", split_axis=1, concat_axis=1, axis_index_groups=along_x, tiled=True
    )
    return blocks.reshape(packed.shape)


def beam_stage(summed, inverse, pair_index, sep_index):
    table = ns_table()
    block = exchange(pack(summed, inverse, table))
    return beam(block, pair_index, sep_index, table)


def local(visibility, day_weight, day_offset, pair_index, sep_index):
    summed, inverse = day_stage(visibility, day_weight, day_offset)
    result = beam_stage(summed, inverse, pair_index, sep_index)
    return result.reshape(BAND, RA_DEV, PAIRS, PIXELS)


def solution(mesh):
    return jax.shard_map(
        local,
        mesh=mesh,
        in_specs=(P("day", None, None, "bl", None), P("day", "bl", None), P(), P(), P()),
        out_specs=P("bl", "day", None, None),
        check_vma=False,
    )
```

```python
import jax
import jax.numpy as jnp
from jax import lax
from jax.experimental import pallas as pl
from jax.experimental.pallas import tpu as pltpu
from jax.sharding import PartitionSpec as P

FREQ = 512
PAIRS = 4
NSEP = 512
PIXELS = 512
HALF = PIXELS // 2
RA = 32
RA_DEV = 2
SAMPLES = 16
DAYS = 16
BASES = 2048
N_BL = 32
BASE_LOC = BASES // N_BL
BAND = FREQ // N_BL
COARSE = 32
FINE = NSEP // COARSE
CHIPS = 8
HELD = 8
SCALE = 128.0
SWAP = [(d, d ^ 1) for d in range(DAYS)]

F32 = jnp.float32
BF16 = jnp.bfloat16
F16 = jnp.float16
MIB = 1 << 20

phase_scale = 2.0 * 3.141592653589793 * 0.3048 / 299.792458


def bins_below(offset, core):
    return 2 * (offset >> 2) + jnp.clip((offset & 3) - 2 * core, 0, 2)


def select_kernel(offset_ref, weight_ref, vis_ref, out_ref, weight_buf, split_buf, sems):
    day = lax.axis_index("day")
    other = 1 - (day & 1)
    offset = offset_ref[day]
    first = bins_below(offset, other)
    load = pltpu.make_async_copy(weight_ref, weight_buf, sems.at[HELD])
    load.start()
    copies = []
    for k in range(HELD):
        owned = first + k
        sample = 4 * (owned >> 1) + 2 * other + (owned & 1) - offset
        copies.append(
            pltpu.make_async_copy(
                vis_ref.at[sample], out_ref.at[owned & (HELD - 1)], sems.at[k]
            )
        )
        copies[-1].start()
    load.wait()
    weight = weight_buf[...]
    high = weight.astype(BF16)
    split_buf[0] = high
    split_buf[1] = (weight - high.astype(F32)).astype(BF16)
    copies.append(pltpu.make_async_copy(split_buf, out_ref.at[HELD], sems.at[HELD + 1]))
    copies[-1].start()
    for copy in copies:
        copy.wait()


def select(day_offset, day_weight, visibility):
    hbm = pl.BlockSpec(memory_space=pl.ANY)
    return pl.pallas_call(
        select_kernel,
        in_specs=[pl.BlockSpec(memory_space=pltpu.SMEM), hbm, hbm],
        out_specs=hbm,
        out_shape=jax.ShapeDtypeStruct((HELD + 1, 2, BASE_LOC, FREQ), BF16),
        scratch_shapes=[
            pltpu.VMEM((BASE_LOC, FREQ), F32),
            pltpu.VMEM((2, BASE_LOC, FREQ), BF16),
            pltpu.SemaphoreType.DMA((HELD + 2,)),
        ],
        compiler_params=pltpu.CompilerParams(vmem_limit_bytes=60 * MIB),
        name="select",
    )(day_offset, day_weight, visibility)


SENDS = (
    ((3, 0), (3, 1), (1, 0), (1, 1)),
    ((5, 0), (5, 1), (7, 0), (7, 1)),
    ((4, 0),),
    ((4, 1),),
    ((2, 0), (2, 1)),
    ((6, 0), (6, 1)),
    ((0, 0), (0, 1)),
)


def chip_kernel(offset_ref, vis_ref, weight_ref, other_ref, *out_refs):
    day = lax.axis_index("day")
    core = day & 1
    chip = day >> 1
    offset = offset_ref[day]
    first = bins_below(offset_ref[day ^ 1], core)
    weight = weight_ref[...] * SCALE
    other_weight = (other_ref[HELD, 0].astype(F32) + other_ref[HELD, 1].astype(F32)) * SCALE
    for out_ref, bins in zip(out_refs, SENDS):
        for at, (distance, which) in enumerate(bins):
            owned = 2 * ((chip + distance) & (CHIPS - 1)) + which
            sample = 4 * (owned >> 1) + 2 * core + which - offset
            valid = jnp.logical_and(sample >= 0, sample < SAMPLES)
            held = jnp.logical_and(owned >= first, owned < first + HELD)
            sample = jnp.clip(sample, 0, SAMPLES - 1)
            own = weight * jnp.where(valid, 1.0, 0.0)
            other = other_weight * jnp.where(held, 1.0, 0.0)
            for x in range(2):
                out_ref[at, x] = (
                    vis_ref[sample, x].astype(F32) * own
                    + other_ref[owned & (HELD - 1), x].astype(F32) * other
                )


def chip_sums(day_offset, visibility, day_weight, other):
    rows = 16
    block = lambda count: pl.BlockSpec((count, 2, rows, FREQ), lambda i: (0, 0, i, 0))
    return pl.pallas_call(
        chip_kernel,
        grid=(BASE_LOC // rows,),
        in_specs=[
            pl.BlockSpec(memory_space=pltpu.SMEM),
            block(SAMPLES),
            pl.BlockSpec((rows, FREQ), lambda i: (i, 0)),
            block(HELD + 1),
        ],
        out_specs=[block(len(bins)) for bins in SENDS],
        out_shape=[
            jax.ShapeDtypeStruct((len(bins), 2, BASE_LOC, FREQ), F32) for bins in SENDS
        ],
        compiler_params=pltpu.CompilerParams(vmem_limit_bytes=16 * MIB),
        name="chip_sums",
    )(day_offset, visibility, day_weight, other)


def reduce_ring(sums):
    def send(values, distance):
        pairs = [
            (2 * y + c, 2 * ((y + distance) % CHIPS) + c) for y in range(CHIPS) for c in range(2)
        ]
        return lax.ppermute(values.astype(F16), "day", pairs)

    near_up, near_down = send(sums[0], 1), send(sums[1], -1)
    far_up, far_down = send(sums[2], 2), send(sums[3], -2)
    middle_up = sums[4] + near_up[:2].astype(F32)
    middle_up = middle_up + jnp.pad(far_up.astype(F32), ((0, 1), (0, 0), (0, 0), (0, 0)))
    middle_down = sums[5] + near_down[:2].astype(F32)
    middle_down = middle_down + jnp.pad(far_down.astype(F32), ((1, 0), (0, 0), (0, 0), (0, 0)))
    last_up, last_down = send(middle_up, 2), send(middle_down, -2)
    return (
        sums[6]
        + near_up[2:].astype(F32)
        + near_down[2:].astype(F32)
        + last_up.astype(F32)
        + last_down.astype(F32)
    )


def table_kernel(cos_a_ref, sin_a_ref, cos_b_ref, sin_b_ref, out_ref):
    cos_b = cos_b_ref[0]
    sin_b = sin_b_ref[0]
    for a in range(COARSE):
        cos_a = cos_a_ref[0, a : a + 1, :]
        sin_a = sin_a_ref[0, a : a + 1, :]
        rows = pl.ds(a * FINE, FINE)
        out_ref[0, rows, :HALF] = (cos_a * cos_b - sin_a * sin_b).astype(BF16)
        out_ref[0, rows, HALF:] = (-(sin_a * cos_b + cos_a * sin_b)).astype(BF16)


def ns_table():
    freq_at = (lax.axis_index("bl") * BAND + jnp.arange(BAND)).astype(F32)
    factor = phase_scale * (800.0 - 400.0 * (freq_at + 0.5) / FREQ)
    sine_dir = -1.0 + 2.0 * (jnp.arange(HALF).astype(F32) + 0.5) / PIXELS
    coarse = (jnp.arange(COARSE) * FINE - NSEP // 2).astype(F32)
    fine = jnp.arange(FINE).astype(F32)
    phase_a = factor[:, None, None] * coarse[None, :, None] * sine_dir[None, None, :]
    phase_b = factor[:, None, None] * fine[None, :, None] * sine_dir[None, None, :]
    spec_a = pl.BlockSpec((1, COARSE, HALF), lambda f: (f, 0, 0))
    spec_b = pl.BlockSpec((1, FINE, HALF), lambda f: (f, 0, 0))
    return pl.pallas_call(
        table_kernel,
        grid=(BAND,),
        in_specs=[spec_a, spec_a, spec_b, spec_b],
        out_specs=pl.BlockSpec((1, NSEP, 2 * HALF), lambda f: (f, 0, 0)),
        out_shape=jax.ShapeDtypeStruct((BAND, NSEP, 2 * HALF), BF16),
        compiler_params=pltpu.CompilerParams(vmem_limit_bytes=60 * MIB),
        cost_estimate=pl.CostEstimate(
            flops=6 * BAND * NSEP * HALF, bytes_accessed=4 * BAND * NSEP * HALF, transcendentals=0
        ),
        name="table",
    )(jnp.cos(phase_a), jnp.sin(phase_a), jnp.cos(phase_b), jnp.sin(phase_b))


def inverse_total(day_offset, day_weight):
    day = lax.axis_index("day")
    core = day & 1
    same = [[2 * y + c for y in range(CHIPS)] for c in range(2)]
    copies = jnp.broadcast_to(day_weight.astype(F16)[None], (CHIPS, BASE_LOC, FREQ))
    weights = lax.all_to_all(
        copies, "day", split_axis=0, concat_axis=0, axis_index_groups=same, tiled=True
    ).astype(F32)
    offsets = jnp.where(core == 0, day_offset[0::2], day_offset[1::2])

    def partial_total(owner):
        sample = (owner * RA_DEV + jnp.arange(RA_DEV))[:, None] - offsets[None, :]
        valid = jnp.logical_and(sample >= 0, sample < SAMPLES).astype(F32)
        return jnp.sum(valid[:, :, None, None] * weights[None], axis=1)

    other = lax.ppermute(partial_total(day ^ 1), "day", SWAP)
    return (1.0 / SCALE) / (partial_total(day) + other)


def pack_blocks(pieces, out_ref, rows):
    lane_group = lax.broadcasted_iota(jnp.int32, (8, 128), 1) // BAND
    for tile in range(FREQ // 128):
        parts = [piece[:, tile * 128 : (tile + 1) * 128] for piece in pieces]
        for step in (4, 2, 1):
            keep = (lane_group & step) == 0
            mixed = list(parts)
            for low in range(8):
                if low & step:
                    continue
                high = low | step
                mixed[low] = jnp.where(keep, parts[low], pltpu.roll(parts[high], step * BAND, 1))
                mixed[high] = jnp.where(
                    keep, pltpu.roll(parts[low], 128 - step * BAND, 1), parts[high]
                )
            parts = mixed
        for group in range(8):
            out_ref[tile * 8 + group, rows, :] = parts[group].astype(BF16)


def pack_kernel(sum_ref, inverse_ref, table_ref, out_ref):
    half = BASE_LOC // 2
    for first in range(0, half, 16):
        for sub in range(0, 16, 8):
            rows = pl.ds(first + sub, 8)
            pieces = []
            for x in range(2):
                for r in range(RA_DEV):
                    for hi in range(2):
                        rows_in = pl.ds(hi * half + first + sub, 8)
                        pieces.append(
                            sum_ref[r, x, rows_in, :] * inverse_ref[r, rows_in, :]
                        )
            pack_blocks(pieces, out_ref, rows)


def pack(summed, inverse, table):
    vmem = pl.BlockSpec(memory_space=pltpu.VMEM)
    return pl.pallas_call(
        pack_kernel,
        in_specs=[vmem, vmem, pl.BlockSpec(memory_space=pl.ANY)],
        out_specs=vmem,
        out_shape=jax.ShapeDtypeStruct((N_BL, BASE_LOC // 2, 128), BF16),
        compiler_params=pltpu.CompilerParams(vmem_limit_bytes=60 * MIB),
        name="pack",
    )(summed, inverse, table)


def beam_kernel(block_ref, pair_ref, sep_ref, table_ref, out_ref, grid_ref, table_buf, sems):
    flat = BASES // 2
    rows = RA_DEV * PAIRS
    loads = []
    for f in range(BAND):
        loads.append(pltpu.make_async_copy(table_ref.at[f], table_buf.at[f], sems.at[f]))
        loads[-1].start()

    turned = block_ref[...].astype(F32).reshape(flat, 128).T
    total = jnp.zeros((2 * rows * BAND, NSEP), F32)
    for hi in range(2):
        picked = [
            turned[(group * 2 + hi) * BAND : (group * 2 + hi + 1) * BAND] for group in range(4)
        ]
        pair = pair_ref[hi : hi + 1, :]
        masked = jnp.concatenate(
            [jnp.where(pair == c, part, 0.0) for part in picked for c in range(PAIRS)], axis=0
        ).astype(BF16)
        sep = sep_ref[:, hi : hi + 1]
        onehot = jnp.where(
            sep == lax.broadcasted_iota(jnp.int32, (flat, NSEP), 1), 1.0, 0.0
        ).astype(BF16)
        total = total + jnp.dot(masked, onehot, preferred_element_type=F32)
    for tile in range(NSEP // 128):
        grid_ref[tile] = total[:, tile * 128 : (tile + 1) * 128]

    flip = (
        lax.broadcasted_iota(jnp.int32, (HALF, HALF), 0)
        + lax.broadcasted_iota(jnp.int32, (HALF, HALF), 1)
        == HALF - 1
    )
    flip = jnp.where(flip, 1.0, 0.0).astype(BF16)
    odd_part = []
    for f in range(BAND):
        cells = jnp.concatenate(
            [
                grid_ref[tile, pl.ds(f, 2 * rows, stride=BAND), :]
                for tile in range(NSEP // 128)
            ],
            axis=1,
        ).astype(BF16)
        loads[f].wait()
        both = jnp.dot(cells, table_buf[f], preferred_element_type=F32)
        cos_part = both[:rows, :HALF]
        sin_part = both[rows:, HALF:]
        even = cos_part + sin_part
        for r in range(RA_DEV):
            out_ref[f, r, :, :HALF] = even[r * PAIRS : (r + 1) * PAIRS]
        odd_part.append(cos_part - sin_part)
    rest = jnp.concatenate(odd_part, axis=0)
    turned = jnp.zeros(rest.shape, F32)
    for _ in range(3):
        piece = rest.astype(BF16)
        rest = rest - piece.astype(F32)
        turned = turned + jnp.dot(piece, flip, preferred_element_type=F32)
    for f in range(BAND):
        for r in range(RA_DEV):
            first = f * rows + r * PAIRS
            out_ref[f, r, :, HALF:] = turned[first : first + PAIRS]


def beam(block, pair_index, sep_index, table):
    flat = BASES // 2
    pair = pair_index.reshape(N_BL, 2, BASE_LOC // 2).transpose(1, 0, 2).reshape(2, flat)
    sep = sep_index.reshape(N_BL, 2, BASE_LOC // 2).transpose(0, 2, 1).reshape(flat, 2)
    vmem = pl.BlockSpec(memory_space=pltpu.VMEM)
    return pl.pallas_call(
        beam_kernel,
        in_specs=[vmem, vmem, vmem, pl.BlockSpec(memory_space=pl.ANY)],
        out_specs=vmem,
        out_shape=jax.ShapeDtypeStruct((BAND, RA_DEV, PAIRS, PIXELS), F32),
        scratch_shapes=[
            pltpu.VMEM((NSEP // 128, 2 * RA_DEV * PAIRS * BAND, 128), F32),
            pltpu.VMEM((BAND, NSEP, 2 * HALF), BF16),
            pltpu.SemaphoreType.DMA((BAND,)),
        ],
        compiler_params=pltpu.CompilerParams(vmem_limit_bytes=58 * MIB),
        name="beam",
    )(block, pair, sep, table)


def day_stage(visibility, day_weight, day_offset):
    visibility, day_weight = visibility[0], day_weight[0]
    inverse = inverse_total(day_offset, day_weight)
    other = lax.ppermute(select(day_offset, day_weight, visibility), "day", SWAP)
    summed = reduce_ring(chip_sums(day_offset, visibility, day_weight, other))
    return summed, inverse


def beam_stage(summed, inverse, pair_index, sep_index):
    table = ns_table()
    packed = pack(summed, inverse, table)
    block = lax.all_to_all(packed, "bl", split_axis=0, concat_axis=0, tiled=True)
    return beam(block, pair_index, sep_index, table)


def local(visibility, day_weight, day_offset, pair_index, sep_index):
    summed, inverse = day_stage(visibility, day_weight, day_offset)
    return beam_stage(summed, inverse, pair_index, sep_index)


def solution(mesh):
    return jax.shard_map(
        local,
        mesh=mesh,
        in_specs=(P("day", None, None, "bl", None), P("day", "bl", None), P(), P(), P()),
        out_specs=P("bl", "day", None, None),
        check_vma=False,
    )
```

```python
import jax
import jax.numpy as jnp
from jax import lax
from jax.experimental import pallas as pl
from jax.experimental.pallas import tpu as pltpu
from jax.sharding import PartitionSpec as P

FREQ = 512
PAIRS = 4
NSEP = 512
PIXELS = 512
HALF = PIXELS // 2
RA = 32
RA_DEV = 2
SAMPLES = 16
DAYS = 16
BASES = 2048
N_BL = 32
BASE_LOC = BASES // N_BL
BAND = FREQ // N_BL
COARSE = 24
FINE = 16
CHIPS = 8
HELD = 8
SCALE = 128.0
SWAP = [(d, d ^ 1) for d in range(DAYS)]

F32 = jnp.float32
BF16 = jnp.bfloat16
F16 = jnp.float16
MIB = 1 << 20

phase_scale = 2.0 * 3.141592653589793 * 0.3048 / 299.792458


def bins_below(offset, core):
    return 2 * (offset >> 2) + jnp.clip((offset & 3) - 2 * core, 0, 2)


def select_kernel(offset_ref, weight_ref, vis_ref, out_ref, weight_buf, sems):
    day = lax.axis_index("day")
    other = 1 - (day & 1)
    offset = offset_ref[day]
    first = bins_below(offset, other)
    load = pltpu.make_async_copy(weight_ref, weight_buf, sems.at[HELD])
    load.start()
    copies = []
    for k in range(HELD):
        owned = first + k
        sample = 4 * (owned >> 1) + 2 * other + (owned & 1) - offset
        copies.append(
            pltpu.make_async_copy(
                vis_ref.at[sample], out_ref.at[owned & (HELD - 1)], sems.at[k]
            )
        )
        copies[-1].start()
    load.wait()
    weight = weight_buf[...]
    high = weight.astype(BF16)
    out_ref[HELD, 0] = high
    out_ref[HELD, 1] = (weight - high.astype(F32)).astype(BF16)
    for copy in copies:
        copy.wait()


def select(day_offset, day_weight, visibility):
    hbm = pl.BlockSpec(memory_space=pl.ANY)
    return pl.pallas_call(
        select_kernel,
        in_specs=[pl.BlockSpec(memory_space=pltpu.SMEM), hbm, hbm],
        out_specs=pl.BlockSpec(memory_space=pltpu.VMEM),
        out_shape=jax.ShapeDtypeStruct((HELD + 1, 2, BASE_LOC, FREQ), BF16),
        scratch_shapes=[
            pltpu.VMEM((BASE_LOC, FREQ), F32),
            pltpu.SemaphoreType.DMA((HELD + 1,)),
        ],
        compiler_params=pltpu.CompilerParams(vmem_limit_bytes=60 * MIB),
        name="select",
    )(day_offset, day_weight, visibility)


SENDS = (
    ((3, 0), (3, 1), (1, 0), (1, 1)),
    ((5, 0), (5, 1), (7, 0), (7, 1)),
    ((4, 0),),
    ((4, 1),),
    ((2, 0), (2, 1)),
    ((6, 0), (6, 1)),
    ((0, 0), (0, 1)),
)


def chip_kernel(offset_ref, vis_ref, weight_ref, other_ref, *out_refs):
    day = lax.axis_index("day")
    core = day & 1
    chip = day >> 1
    offset = offset_ref[day]
    first = bins_below(offset_ref[day ^ 1], core)
    weight = weight_ref[...] * SCALE
    other_weight = (other_ref[HELD, 0].astype(F32) + other_ref[HELD, 1].astype(F32)) * SCALE
    for out_ref, bins in zip(out_refs, SENDS):
        for at, (distance, which) in enumerate(bins):
            owned = 2 * ((chip + distance) & (CHIPS - 1)) + which
            sample = 4 * (owned >> 1) + 2 * core + which - offset
            valid = jnp.logical_and(sample >= 0, sample < SAMPLES)
            held = jnp.logical_and(owned >= first, owned < first + HELD)
            sample = jnp.clip(sample, 0, SAMPLES - 1)
            own = weight * jnp.where(valid, 1.0, 0.0)
            other = other_weight * jnp.where(held, 1.0, 0.0)
            for x in range(2):
                out_ref[at, x] = (
                    vis_ref[sample, x].astype(F32) * own
                    + other_ref[owned & (HELD - 1), x].astype(F32) * other
                )


def chip_sums(day_offset, visibility, day_weight, other):
    rows = 16
    block = lambda count: pl.BlockSpec((count, 2, rows, FREQ), lambda i: (0, 0, i, 0))
    return pl.pallas_call(
        chip_kernel,
        grid=(BASE_LOC // rows,),
        in_specs=[
            pl.BlockSpec(memory_space=pltpu.SMEM),
            block(SAMPLES),
            pl.BlockSpec((rows, FREQ), lambda i: (i, 0)),
            block(HELD + 1),
        ],
        out_specs=[block(len(bins)) for bins in SENDS],
        out_shape=[
            jax.ShapeDtypeStruct((len(bins), 2, BASE_LOC, FREQ), F32) for bins in SENDS
        ],
        compiler_params=pltpu.CompilerParams(vmem_limit_bytes=16 * MIB),
        name="chip_sums",
    )(day_offset, visibility, day_weight, other)


def send(values, distance):
    pairs = [
        (2 * y + c, 2 * ((y + distance) % CHIPS) + c) for y in range(CHIPS) for c in range(2)
    ]
    return lax.ppermute(values.astype(F16), "day", pairs)


def reduce_ring(sums, late):
    near_up, near_down = send(sums[0], 1), send(sums[1], -1)
    far_up, far_down = send(sums[2], 2), send(sums[3], -2)
    middle_up = sums[4] + near_up[:2].astype(F32)
    middle_up = middle_up + jnp.pad(far_up.astype(F32), ((0, 1), (0, 0), (0, 0), (0, 0)))
    middle_down = sums[5] + near_down[:2].astype(F32)
    middle_down = middle_down + jnp.pad(far_down.astype(F32), ((1, 0), (0, 0), (0, 0), (0, 0)))
    middle_up, middle_down = middle_up.astype(F16), middle_down.astype(F16)
    late = lax.optimization_barrier((*late, middle_up, middle_down))[:-2]
    last_up, last_down = send(middle_up, 2), send(middle_down, -2)
    summed = (
        sums[6]
        + near_up[2:].astype(F32)
        + near_down[2:].astype(F32)
        + last_up.astype(F32)
        + last_down.astype(F32)
    )
    return summed, late


def gather_weights(day_weight):
    same = [[2 * y + c for y in range(CHIPS)] for c in range(2)]
    copies = jnp.broadcast_to(day_weight.astype(F16)[None], (CHIPS, BASE_LOC, FREQ))
    return lax.all_to_all(
        copies, "day", split_axis=0, concat_axis=0, axis_index_groups=same, tiled=True
    )


def inverse_total(day_offset, weights):
    day = lax.axis_index("day")
    offsets = jnp.where((day & 1) == 0, day_offset[0::2], day_offset[1::2])
    weights = weights.astype(F32)

    def partial_total(owner):
        sample = (owner * RA_DEV + jnp.arange(RA_DEV))[:, None] - offsets[None, :]
        valid = jnp.logical_and(sample >= 0, sample < SAMPLES).astype(F32)
        return jnp.sum(valid[:, :, None, None] * weights[None], axis=1)

    other = lax.ppermute(partial_total(day ^ 1), "day", SWAP)
    return (1.0 / SCALE) / (partial_total(day) + other)


def base_angles(freq_at):
    factor = phase_scale * (800.0 - 400.0 * (freq_at + 0.5) / FREQ)
    sine_dir = -1.0 + 2.0 * (jnp.arange(HALF).astype(F32) + 0.5) / PIXELS
    separation = jnp.concatenate([jnp.arange(COARSE) * FINE, jnp.arange(FINE)]).astype(F32)
    phase = factor[:, None, None] * separation[None, :, None] * sine_dir[None, None, :]
    return jnp.cos(phase), jnp.sin(phase)


def pack_blocks(pieces, out_ref, rows):
    lane_group = lax.broadcasted_iota(jnp.int32, (8, 128), 1) // BAND
    for tile in range(FREQ // 128):
        parts = [piece[:, tile * 128 : (tile + 1) * 128] for piece in pieces]
        for step in (4, 2, 1):
            keep = (lane_group & step) == 0
            mixed = list(parts)
            for low in range(8):
                if low & step:
                    continue
                high = low | step
                mixed[low] = jnp.where(keep, parts[low], pltpu.roll(parts[high], step * BAND, 1))
                mixed[high] = jnp.where(
                    keep, pltpu.roll(parts[low], 128 - step * BAND, 1), parts[high]
                )
            parts = mixed
        for group in range(8):
            out_ref[tile * 8 + group, rows, :] = parts[group].astype(BF16)


def pack_kernel(sum_ref, inverse_ref, out_ref):
    half = BASE_LOC // 2
    for first in range(0, half, 16):
        for sub in range(0, 16, 8):
            rows = pl.ds(first + sub, 8)
            pieces = []
            for x in range(2):
                for r in range(RA_DEV):
                    for hi in range(2):
                        rows_in = pl.ds(hi * half + first + sub, 8)
                        pieces.append(
                            sum_ref[r, x, rows_in, :] * inverse_ref[r, rows_in, :]
                        )
            pack_blocks(pieces, out_ref, rows)


def pack(summed, inverse):
    vmem = pl.BlockSpec(memory_space=pltpu.VMEM)
    return pl.pallas_call(
        pack_kernel,
        in_specs=[vmem, vmem],
        out_specs=vmem,
        out_shape=jax.ShapeDtypeStruct((N_BL, BASE_LOC // 2, 128), BF16),
        compiler_params=pltpu.CompilerParams(vmem_limit_bytes=16 * MIB),
        name="pack",
    )(summed, inverse)


def beam_kernel(block_ref, pair_ref, sep_ref, cos_ref, sin_ref, out_ref, grid_ref, table_buf):
    flat = BASES // 2
    rows = RA_DEV * PAIRS

    turned = block_ref[...].astype(F32).reshape(flat, 128).T
    total = jnp.zeros((2 * rows * BAND, NSEP), F32)
    for hi in range(2):
        picked = [
            turned[(group * 2 + hi) * BAND : (group * 2 + hi + 1) * BAND] for group in range(4)
        ]
        pair = pair_ref[hi : hi + 1, :]
        masked = jnp.concatenate(
            [jnp.where(pair == c, part, 0.0) for part in picked for c in range(PAIRS)], axis=0
        ).astype(BF16)
        sep = sep_ref[:, hi : hi + 1]
        column = jnp.where(
            sep >= NSEP // 2, sep - NSEP // 2, jnp.where(sep == 0, NSEP // 2, NSEP - sep)
        )
        onehot = jnp.where(
            column == lax.broadcasted_iota(jnp.int32, (flat, NSEP), 1), 1.0, 0.0
        ).astype(BF16)
        total = total + jnp.dot(masked, onehot, preferred_element_type=F32)
    for tile in range(NSEP // 128):
        grid_ref[tile] = total[:, tile * 128 : (tile + 1) * 128]

    flip = (
        lax.broadcasted_iota(jnp.int32, (HALF, HALF), 0)
        + lax.broadcasted_iota(jnp.int32, (HALF, HALF), 1)
        == HALF - 1
    )
    flip = jnp.where(flip, 1.0, 0.0).astype(BF16)
    odd_part = []
    edge = NSEP // 2 // FINE
    for f in range(BAND):
        cos_b = cos_ref[f, COARSE:, :]
        sin_b = sin_ref[f, COARSE:, :]
        for a in range(edge):
            cos_a = cos_ref[f, a : a + 1, :]
            sin_a = sin_ref[f, a : a + 1, :]
            at = pl.ds(a * FINE, FINE)
            table_buf[f, at, :HALF] = (cos_a * cos_b - sin_a * sin_b).astype(BF16)
            table_buf[f, at, HALF:] = (-(sin_a * cos_b + cos_a * sin_b)).astype(BF16)
        tiles = [grid_ref[tile, pl.ds(f, 2 * rows, stride=BAND), :] for tile in range(4)]
        cells = jnp.concatenate(
            [jnp.concatenate(tiles[:2], axis=1), jnp.concatenate(tiles[2:], axis=1)], axis=0
        ).astype(BF16)
        lone = tiles[2][:, :1]
        both = jnp.dot(cells, table_buf[f], preferred_element_type=F32)
        edge_cos = cos_ref[f, edge : edge + 1, :].astype(BF16).astype(F32)
        edge_sin = sin_ref[f, edge : edge + 1, :].astype(BF16).astype(F32)
        cos_part = both[:rows, :HALF] + both[2 * rows : 3 * rows, :HALF]
        cos_part = cos_part + lone[:rows] * (edge_cos - 1.0)
        sin_part = both[rows : 2 * rows, HALF:] - both[3 * rows :, HALF:]
        sin_part = sin_part + lone[rows:] * edge_sin
        even = cos_part + sin_part
        for r in range(RA_DEV):
            out_ref[f, r, :, :HALF] = even[r * PAIRS : (r + 1) * PAIRS]
        odd_part.append(cos_part - sin_part)
    rest = jnp.concatenate(odd_part, axis=0)
    turned = jnp.zeros(rest.shape, F32)
    for _ in range(3):
        piece = rest.astype(BF16)
        rest = rest - piece.astype(F32)
        turned = turned + jnp.dot(piece, flip, preferred_element_type=F32)
    for f in range(BAND):
        for r in range(RA_DEV):
            first = f * rows + r * PAIRS
            out_ref[f, r, :, HALF:] = turned[first : first + PAIRS]


def beam(block, pair_index, sep_index, angles):
    flat = BASES // 2
    pair = pair_index.reshape(N_BL, 2, BASE_LOC // 2).transpose(1, 0, 2).reshape(2, flat)
    sep = sep_index.reshape(N_BL, 2, BASE_LOC // 2).transpose(0, 2, 1).reshape(flat, 2)
    vmem = pl.BlockSpec(memory_space=pltpu.VMEM)
    return pl.pallas_call(
        beam_kernel,
        in_specs=[vmem] * 5,
        out_specs=vmem,
        out_shape=jax.ShapeDtypeStruct((BAND, RA_DEV, PAIRS, PIXELS), F32),
        scratch_shapes=[
            pltpu.VMEM((NSEP // 128, 2 * RA_DEV * PAIRS * BAND, 128), F32),
            pltpu.VMEM((BAND, NSEP // 2, 2 * HALF), BF16),
        ],
        compiler_params=pltpu.CompilerParams(vmem_limit_bytes=32 * MIB),
        name="beam",
    )(block, pair, sep, *angles)


def day_stage(visibility, day_weight, day_offset, freq_at):
    visibility, day_weight = visibility[0], day_weight[0]
    other = lax.ppermute(select(day_offset, day_weight, visibility), "day", SWAP)
    weights = gather_weights(day_weight)
    sums = chip_sums(day_offset, visibility, day_weight, other)
    summed, (weights, freq_at) = reduce_ring(sums, (weights, freq_at))
    return summed, inverse_total(day_offset, weights), freq_at


def beam_stage(summed, inverse, pair_index, sep_index, freq_at):
    angles = base_angles(freq_at)
    packed = pack(summed, inverse)
    block = lax.all_to_all(packed, "bl", split_axis=0, concat_axis=0, tiled=True)
    return beam(block, pair_index, sep_index, angles)


def local(visibility, day_weight, day_offset, pair_index, sep_index):
    freq_at = (lax.axis_index("bl") * BAND + jnp.arange(BAND)).astype(F32)
    summed, inverse, freq_at = day_stage(visibility, day_weight, day_offset, freq_at)
    return beam_stage(summed, inverse, pair_index, sep_index, freq_at)


def solution(mesh):
    return jax.shard_map(
        local,
        mesh=mesh,
        in_specs=(P("day", None, None, "bl", None), P("day", "bl", None), P(), P(), P()),
        out_specs=P("bl", "day", None, None),
        check_vma=False,
    )
```

```python
import jax
import jax.numpy as jnp
from jax import lax
from jax.experimental import pallas as pl
from jax.experimental.pallas import tpu as pltpu
from jax.sharding import PartitionSpec as P

FREQ = 512
PAIRS = 4
NSEP = 512
PIXELS = 512
HALF = PIXELS // 2
RA = 32
RA_DEV = 2
SAMPLES = 16
DAYS = 16
BASES = 2048
N_BL = 32
BASE_LOC = BASES // N_BL
BAND = FREQ // N_BL
COARSE = 24
FINE = 16
CHIPS = 8
HELD = 8
SCALE = 128.0
SWAP = [(d, d ^ 1) for d in range(DAYS)]

F32 = jnp.float32
BF16 = jnp.bfloat16
F16 = jnp.float16
MIB = 1 << 20

phase_scale = 2.0 * 3.141592653589793 * 0.3048 / 299.792458


def bins_below(offset, core):
    return 2 * (offset >> 2) + jnp.clip((offset & 3) - 2 * core, 0, 2)


def select_kernel(offset_ref, weight_ref, vis_ref, out_ref, weight_buf, sems):
    day = lax.axis_index("day")
    other = 1 - (day & 1)
    offset = offset_ref[day]
    first = bins_below(offset, other)
    load = pltpu.make_async_copy(weight_ref, weight_buf, sems.at[HELD])
    load.start()
    copies = []
    for k in range(HELD):
        owned = first + k
        sample = 4 * (owned >> 1) + 2 * other + (owned & 1) - offset
        copies.append(
            pltpu.make_async_copy(
                vis_ref.at[sample], out_ref.at[owned & (HELD - 1)], sems.at[k]
            )
        )
        copies[-1].start()
    load.wait()
    weight = weight_buf[...]
    high = weight.astype(BF16)
    out_ref[HELD, 0] = high
    out_ref[HELD, 1] = (weight - high.astype(F32)).astype(BF16)
    for copy in copies:
        copy.wait()


def select(day_offset, day_weight, visibility):
    hbm = pl.BlockSpec(memory_space=pl.ANY)
    return pl.pallas_call(
        select_kernel,
        in_specs=[pl.BlockSpec(memory_space=pltpu.SMEM), hbm, hbm],
        out_specs=pl.BlockSpec(memory_space=pltpu.VMEM),
        out_shape=jax.ShapeDtypeStruct((HELD + 1, 2, BASE_LOC, FREQ), BF16),
        scratch_shapes=[
            pltpu.VMEM((BASE_LOC, FREQ), F32),
            pltpu.SemaphoreType.DMA((HELD + 1,)),
        ],
        compiler_params=pltpu.CompilerParams(vmem_limit_bytes=60 * MIB),
        name="select",
    )(day_offset, day_weight, visibility)


def chip_kernel(offset_ref, vis_ref, weight_ref, other_ref, out_ref):
    day = lax.axis_index("day")
    core = day & 1
    offset = offset_ref[day]
    first = bins_below(offset_ref[day ^ 1], core)
    weight = weight_ref[...] * SCALE
    other_weight = (other_ref[HELD, 0].astype(F32) + other_ref[HELD, 1].astype(F32)) * SCALE
    for owned in range(2 * CHIPS):
        sample = 4 * (owned >> 1) + 2 * core + (owned & 1) - offset
        valid = jnp.logical_and(sample >= 0, sample < SAMPLES)
        held = jnp.logical_and(owned >= first, owned < first + HELD)
        sample = jnp.clip(sample, 0, SAMPLES - 1)
        own = weight * jnp.where(valid, 1.0, 0.0)
        other = other_weight * jnp.where(held, 1.0, 0.0)
        for x in range(2):
            out_ref[owned, x] = (
                vis_ref[sample, x].astype(F32) * own
                + other_ref[owned & (HELD - 1), x].astype(F32) * other
            )


def chip_sums(day_offset, visibility, day_weight, other):
    rows = 16
    block = lambda count: pl.BlockSpec((count, 2, rows, FREQ), lambda i: (0, 0, i, 0))
    return pl.pallas_call(
        chip_kernel,
        grid=(BASE_LOC // rows,),
        in_specs=[
            pl.BlockSpec(memory_space=pltpu.SMEM),
            block(SAMPLES),
            pl.BlockSpec((rows, FREQ), lambda i: (i, 0)),
            block(HELD + 1),
        ],
        out_specs=block(2 * CHIPS),
        out_shape=jax.ShapeDtypeStruct((2 * CHIPS, 2, BASE_LOC, FREQ), F32),
        compiler_params=pltpu.CompilerParams(vmem_limit_bytes=16 * MIB),
        name="chip_sums",
    )(day_offset, visibility, day_weight, other)


def along_day(blocks):
    same = [[2 * y + c for y in range(CHIPS)] for c in range(2)]
    return lax.all_to_all(
        blocks, "day", split_axis=0, concat_axis=0, axis_index_groups=same, tiled=True
    )


def gather_weights(day_weight):
    return along_day(jnp.broadcast_to(day_weight.astype(F16)[None], (CHIPS, BASE_LOC, FREQ)))


def partial_totals(day_offset, weights):
    day = lax.axis_index("day")
    offsets = jnp.where((day & 1) == 0, day_offset[0::2], day_offset[1::2])
    weights = weights.astype(F32)
    totals = []
    for owner in (day, day ^ 1):
        sample = (owner * RA_DEV + jnp.arange(RA_DEV))[:, None] - offsets[None, :]
        valid = jnp.logical_and(sample >= 0, sample < SAMPLES).astype(F32)
        totals.append(jnp.sum(valid[:, :, None, None] * weights[None], axis=1))
    return totals


def base_angles(freq_at):
    factor = phase_scale * (800.0 - 400.0 * (freq_at + 0.5) / FREQ)
    sine_dir = -1.0 + 2.0 * (jnp.arange(HALF).astype(F32) + 0.5) / PIXELS
    separation = jnp.concatenate([jnp.arange(COARSE) * FINE, jnp.arange(FINE)]).astype(F32)
    phase = factor[:, None, None] * separation[None, :, None] * sine_dir[None, None, :]
    return jnp.cos(phase), jnp.sin(phase)


def pack_blocks(pieces, out_ref, rows):
    lane_group = lax.broadcasted_iota(jnp.int32, (8, 128), 1) // BAND
    for tile in range(FREQ // 128):
        parts = [piece[:, tile * 128 : (tile + 1) * 128] for piece in pieces]
        for step in (4, 2, 1):
            keep = (lane_group & step) == 0
            mixed = list(parts)
            for low in range(8):
                if low & step:
                    continue
                high = low | step
                mixed[low] = jnp.where(keep, parts[low], pltpu.roll(parts[high], step * BAND, 1))
                mixed[high] = jnp.where(
                    keep, pltpu.roll(parts[low], 128 - step * BAND, 1), parts[high]
                )
            parts = mixed
        for group in range(8):
            out_ref[tile * 8 + group, rows, :] = parts[group].astype(BF16)


def pack_kernel(sum_ref, inverse_ref, out_ref):
    half = BASE_LOC // 2
    for first in range(0, half, 16):
        for sub in range(0, 16, 8):
            rows = pl.ds(first + sub, 8)
            pieces = []
            for x in range(2):
                for r in range(RA_DEV):
                    for hi in range(2):
                        rows_in = pl.ds(hi * half + first + sub, 8)
                        pieces.append(
                            sum_ref[r, x, rows_in, :] * inverse_ref[r, rows_in, :]
                        )
            pack_blocks(pieces, out_ref, rows)


def pack(summed, inverse):
    vmem = pl.BlockSpec(memory_space=pltpu.VMEM)
    return pl.pallas_call(
        pack_kernel,
        in_specs=[vmem, vmem],
        out_specs=vmem,
        out_shape=jax.ShapeDtypeStruct((N_BL, BASE_LOC // 2, 128), BF16),
        compiler_params=pltpu.CompilerParams(vmem_limit_bytes=16 * MIB),
        name="pack",
    )(summed, inverse)


def beam_kernel(block_ref, pair_ref, sep_ref, cos_ref, sin_ref, out_ref, grid_ref, table_buf):
    flat = BASES // 2
    rows = RA_DEV * PAIRS

    turned = block_ref[...].astype(F32).reshape(flat, 128).T
    total = jnp.zeros((2 * rows * BAND, NSEP), F32)
    for hi in range(2):
        picked = [
            turned[(group * 2 + hi) * BAND : (group * 2 + hi + 1) * BAND] for group in range(4)
        ]
        pair = pair_ref[hi : hi + 1, :]
        masked = jnp.concatenate(
            [jnp.where(pair == c, part, 0.0) for part in picked for c in range(PAIRS)], axis=0
        ).astype(BF16)
        sep = sep_ref[:, hi : hi + 1]
        column = jnp.where(
            sep >= NSEP // 2, sep - NSEP // 2, jnp.where(sep == 0, NSEP // 2, NSEP - sep)
        )
        onehot = jnp.where(
            column == lax.broadcasted_iota(jnp.int32, (flat, NSEP), 1), 1.0, 0.0
        ).astype(BF16)
        total = total + jnp.dot(masked, onehot, preferred_element_type=F32)
    for tile in range(NSEP // 128):
        grid_ref[tile] = total[:, tile * 128 : (tile + 1) * 128]

    flip = (
        lax.broadcasted_iota(jnp.int32, (HALF, HALF), 0)
        + lax.broadcasted_iota(jnp.int32, (HALF, HALF), 1)
        == HALF - 1
    )
    flip = jnp.where(flip, 1.0, 0.0).astype(BF16)
    odd_part = []
    edge = NSEP // 2 // FINE
    for f in range(BAND):
        cos_b = cos_ref[f, COARSE:, :]
        sin_b = sin_ref[f, COARSE:, :]
        for a in range(edge):
            cos_a = cos_ref[f, a : a + 1, :]
            sin_a = sin_ref[f, a : a + 1, :]
            at = pl.ds(a * FINE, FINE)
            table_buf[f, at, :HALF] = (cos_a * cos_b - sin_a * sin_b).astype(BF16)
            table_buf[f, at, HALF:] = (-(sin_a * cos_b + cos_a * sin_b)).astype(BF16)
        tiles = [grid_ref[tile, pl.ds(f, 2 * rows, stride=BAND), :] for tile in range(4)]
        cells = jnp.concatenate(
            [jnp.concatenate(tiles[:2], axis=1), jnp.concatenate(tiles[2:], axis=1)], axis=0
        ).astype(BF16)
        lone = tiles[2][:, :1]
        both = jnp.dot(cells, table_buf[f], preferred_element_type=F32)
        edge_cos = cos_ref[f, edge : edge + 1, :].astype(BF16).astype(F32)
        edge_sin = sin_ref[f, edge : edge + 1, :].astype(BF16).astype(F32)
        cos_part = both[:rows, :HALF] + both[2 * rows : 3 * rows, :HALF]
        cos_part = cos_part + lone[:rows] * (edge_cos - 1.0)
        sin_part = both[rows : 2 * rows, HALF:] - both[3 * rows :, HALF:]
        sin_part = sin_part + lone[rows:] * edge_sin
        even = cos_part + sin_part
        for r in range(RA_DEV):
            out_ref[f, r, :, :HALF] = even[r * PAIRS : (r + 1) * PAIRS]
        odd_part.append(cos_part - sin_part)
    rest = jnp.concatenate(odd_part, axis=0)
    turned = jnp.zeros(rest.shape, F32)
    for _ in range(3):
        piece = rest.astype(BF16)
        rest = rest - piece.astype(F32)
        turned = turned + jnp.dot(piece, flip, preferred_element_type=F32)
    for f in range(BAND):
        for r in range(RA_DEV):
            first = f * rows + r * PAIRS
            out_ref[f, r, :, HALF:] = turned[first : first + PAIRS]


def beam(block, pair_index, sep_index, angles):
    flat = BASES // 2
    pair = pair_index.reshape(N_BL, 2, BASE_LOC // 2).transpose(1, 0, 2).reshape(2, flat)
    sep = sep_index.reshape(N_BL, 2, BASE_LOC // 2).transpose(0, 2, 1).reshape(flat, 2)
    vmem = pl.BlockSpec(memory_space=pltpu.VMEM)
    return pl.pallas_call(
        beam_kernel,
        in_specs=[vmem] * 5,
        out_specs=vmem,
        out_shape=jax.ShapeDtypeStruct((BAND, RA_DEV, PAIRS, PIXELS), F32),
        scratch_shapes=[
            pltpu.VMEM((NSEP // 128, 2 * RA_DEV * PAIRS * BAND, 128), F32),
            pltpu.VMEM((BAND, NSEP // 2, 2 * HALF), BF16),
        ],
        compiler_params=pltpu.CompilerParams(vmem_limit_bytes=32 * MIB),
        name="beam",
    )(block, pair, sep, *angles)


def day_stage(visibility, day_weight, day_offset, freq_at):
    visibility, day_weight = visibility[0], day_weight[0]
    other = lax.ppermute(select(day_offset, day_weight, visibility), "day", SWAP)
    weights = gather_weights(day_weight)
    sums = chip_sums(day_offset, visibility, day_weight, other).astype(F16)
    weights, freq_at, _ = lax.optimization_barrier((weights, freq_at, sums))
    sums = along_day(sums.reshape(CHIPS, RA_DEV, 2, BASE_LOC, FREQ))
    mine, theirs = partial_totals(day_offset, weights)
    inverse = (1.0 / SCALE) / (mine + lax.ppermute(theirs, "day", SWAP))
    return jnp.sum(sums.astype(F32), axis=0), inverse, freq_at


def beam_stage(summed, inverse, pair_index, sep_index, freq_at):
    angles = base_angles(freq_at)
    packed = pack(summed, inverse)
    block = lax.all_to_all(packed, "bl", split_axis=0, concat_axis=0, tiled=True)
    return beam(block, pair_index, sep_index, angles)


def local(visibility, day_weight, day_offset, pair_index, sep_index):
    freq_at = (lax.axis_index("bl") * BAND + jnp.arange(BAND)).astype(F32)
    summed, inverse, freq_at = day_stage(visibility, day_weight, day_offset, freq_at)
    return beam_stage(summed, inverse, pair_index, sep_index, freq_at)


def solution(mesh):
    return jax.shard_map(
        local,
        mesh=mesh,
        in_specs=(P("day", None, None, "bl", None), P("day", "bl", None), P(), P(), P()),
        out_specs=P("bl", "day", None, None),
        check_vma=False,
    )
```

```python
import jax
import jax.numpy as jnp
from jax import lax
from jax.experimental import pallas as pl
from jax.experimental.pallas import tpu as pltpu
from jax.sharding import PartitionSpec as P

FREQ = 512
PAIRS = 4
NSEP = 512
PIXELS = 512
HALF = PIXELS // 2
RA = 32
RA_DEV = 2
SAMPLES = 16
DAYS = 16
BASES = 2048
N_BL = 32
BASE_LOC = BASES // N_BL
BAND = FREQ // N_BL
COARSE = 24
FINE = 16
CHIPS = 8
HELD = 8
SCALE = 128.0
SWAP = [(d, d ^ 1) for d in range(DAYS)]

F32 = jnp.float32
BF16 = jnp.bfloat16
F16 = jnp.float16
MIB = 1 << 20

phase_scale = 2.0 * 3.141592653589793 * 0.3048 / 299.792458


def bins_below(offset, core):
    return 2 * (offset >> 2) + jnp.clip((offset & 3) - 2 * core, 0, 2)


def select_kernel(offset_ref, weight_ref, vis_ref, out_ref, weight_buf, held_buf, sems):
    day = lax.axis_index("day")
    other = 1 - (day & 1)
    offset = offset_ref[day]
    first = bins_below(offset, other)
    load = pltpu.make_async_copy(weight_ref, weight_buf, sems.at[HELD])
    load.start()
    loads, stores = [], []
    for k in range(HELD):
        owned = first + k
        sample = 4 * (owned >> 1) + 2 * other + (owned & 1) - offset
        slot = owned & (HELD - 1)
        loads.append(pltpu.make_async_copy(vis_ref.at[sample], held_buf.at[k], sems.at[k]))
        loads[-1].start()
        stores.append(
            pltpu.make_async_copy(held_buf.at[k], out_ref.at[slot], sems.at[HELD + 1 + k])
        )
    load.wait()
    weight = weight_buf[...]
    high = weight.astype(BF16)
    held_buf[HELD, 0] = high
    held_buf[HELD, 1] = (weight - high.astype(F32)).astype(BF16)
    stores.append(
        pltpu.make_async_copy(held_buf.at[HELD], out_ref.at[HELD], sems.at[2 * HELD + 1])
    )
    stores[-1].start()
    for k in range(HELD):
        loads[k].wait()
        stores[k].start()
    for store in stores:
        store.wait()


def select(day_offset, day_weight, visibility):
    hbm = pl.BlockSpec(memory_space=pl.ANY)
    return pl.pallas_call(
        select_kernel,
        in_specs=[pl.BlockSpec(memory_space=pltpu.SMEM), hbm, hbm],
        out_specs=hbm,
        out_shape=jax.ShapeDtypeStruct((HELD + 1, 2, BASE_LOC, FREQ), BF16),
        scratch_shapes=[
            pltpu.VMEM((BASE_LOC, FREQ), F32),
            pltpu.VMEM((HELD + 1, 2, BASE_LOC, FREQ), BF16),
            pltpu.SemaphoreType.DMA((2 * HELD + 2,)),
        ],
        compiler_params=pltpu.CompilerParams(vmem_limit_bytes=60 * MIB),
        name="select",
    )(day_offset, day_weight, visibility)


SENDS = (
    ((3, 0), (3, 1), (1, 0), (1, 1)),
    ((5, 0), (5, 1), (7, 0), (7, 1)),
    ((4, 0),),
    ((4, 1),),
    ((2, 0), (2, 1)),
    ((6, 0), (6, 1)),
    ((0, 0), (0, 1)),
)


def chip_kernel(offset_ref, vis_ref, weight_ref, other_ref, *out_refs):
    day = lax.axis_index("day")
    core = day & 1
    chip = day >> 1
    offset = offset_ref[day]
    first = bins_below(offset_ref[day ^ 1], core)
    weight = weight_ref[...] * SCALE
    other_weight = (other_ref[HELD, 0].astype(F32) + other_ref[HELD, 1].astype(F32)) * SCALE
    for out_ref, bins in zip(out_refs, SENDS):
        for at, (distance, which) in enumerate(bins):
            owned = 2 * ((chip + distance) & (CHIPS - 1)) + which
            sample = 4 * (owned >> 1) + 2 * core + which - offset
            valid = jnp.logical_and(sample >= 0, sample < SAMPLES)
            held = jnp.logical_and(owned >= first, owned < first + HELD)
            sample = jnp.clip(sample, 0, SAMPLES - 1)
            own = weight * jnp.where(valid, 1.0, 0.0)
            other = other_weight * jnp.where(held, 1.0, 0.0)
            for x in range(2):
                out_ref[at, x] = (
                    vis_ref[sample, x].astype(F32) * own
                    + other_ref[owned & (HELD - 1), x].astype(F32) * other
                )


def chip_sums(day_offset, visibility, day_weight, other):
    rows = 16
    block = lambda count: pl.BlockSpec((count, 2, rows, FREQ), lambda i: (0, 0, i, 0))
    return pl.pallas_call(
        chip_kernel,
        grid=(BASE_LOC // rows,),
        in_specs=[
            pl.BlockSpec(memory_space=pltpu.SMEM),
            block(SAMPLES),
            pl.BlockSpec((rows, FREQ), lambda i: (i, 0)),
            block(HELD + 1),
        ],
        out_specs=[block(len(bins)) for bins in SENDS],
        out_shape=[
            jax.ShapeDtypeStruct((len(bins), 2, BASE_LOC, FREQ), F32) for bins in SENDS
        ],
        compiler_params=pltpu.CompilerParams(vmem_limit_bytes=16 * MIB),
        name="chip_sums",
    )(day_offset, visibility, day_weight, other)


def send(values, distance):
    pairs = [
        (2 * y + c, 2 * ((y + distance) % CHIPS) + c) for y in range(CHIPS) for c in range(2)
    ]
    return lax.ppermute(values, "day", pairs)


def reduce_ring(sums, late):
    first = lax.optimization_barrier([part.astype(F16) for part in sums[:4]])
    near_up, near_down = send(first[0], 1), send(first[1], -1)
    far_up, far_down = send(first[2], 2), send(first[3], -2)
    middle_up = sums[4] + near_up[:2].astype(F32)
    middle_up = middle_up + jnp.pad(far_up.astype(F32), ((0, 1), (0, 0), (0, 0), (0, 0)))
    middle_down = sums[5] + near_down[:2].astype(F32)
    middle_down = middle_down + jnp.pad(far_down.astype(F32), ((1, 0), (0, 0), (0, 0), (0, 0)))
    middle_up, middle_down = middle_up.astype(F16), middle_down.astype(F16)
    last_up, last_down = send(middle_up, 2), send(middle_down, -2)
    late = lax.optimization_barrier((late, last_up))[0]
    summed = (
        sums[6]
        + near_up[2:].astype(F32)
        + near_down[2:].astype(F32)
        + last_up.astype(F32)
        + last_down.astype(F32)
    )
    return summed, late


def gather_weights(day_weight):
    same = [[2 * y + c for y in range(CHIPS)] for c in range(2)]
    copies = jnp.broadcast_to(day_weight.astype(F16)[None], (CHIPS, BASE_LOC, FREQ))
    return lax.all_to_all(
        copies, "day", split_axis=0, concat_axis=0, axis_index_groups=same, tiled=True
    )


def inverse_total(day_offset, weights):
    day = lax.axis_index("day")
    offsets = jnp.where((day & 1) == 0, day_offset[0::2], day_offset[1::2])
    weights = weights.astype(F32)

    def partial_total(owner):
        sample = (owner * RA_DEV + jnp.arange(RA_DEV))[:, None] - offsets[None, :]
        valid = jnp.logical_and(sample >= 0, sample < SAMPLES).astype(F32)
        return jnp.sum(valid[:, :, None, None] * weights[None], axis=1)

    other = lax.ppermute(partial_total(day ^ 1), "day", SWAP)
    return (1.0 / SCALE) / (partial_total(day) + other)


def base_angles(freq_at):
    factor = phase_scale * (800.0 - 400.0 * (freq_at + 0.5) / FREQ)
    sine_dir = -1.0 + 2.0 * (jnp.arange(HALF).astype(F32) + 0.5) / PIXELS
    separation = jnp.concatenate([jnp.arange(COARSE) * FINE, jnp.arange(FINE)]).astype(F32)
    phase = factor[:, None, None] * separation[None, :, None] * sine_dir[None, None, :]
    return jnp.cos(phase), jnp.sin(phase)


def pack_blocks(pieces, out_ref, rows):
    lane_group = lax.broadcasted_iota(jnp.int32, (8, 128), 1) // BAND
    for tile in range(FREQ // 128):
        parts = [piece[:, tile * 128 : (tile + 1) * 128] for piece in pieces]
        for step in (4, 2, 1):
            keep = (lane_group & step) == 0
            mixed = list(parts)
            for low in range(8):
                if low & step:
                    continue
                high = low | step
                mixed[low] = jnp.where(keep, parts[low], pltpu.roll(parts[high], step * BAND, 1))
                mixed[high] = jnp.where(
                    keep, pltpu.roll(parts[low], 128 - step * BAND, 1), parts[high]
                )
            parts = mixed
        for group in range(8):
            out_ref[tile * 8 + group, rows, :] = parts[group].astype(BF16)


def pack_kernel(sum_ref, inverse_ref, out_ref):
    half = BASE_LOC // 2
    for first in range(0, half, 16):
        for sub in range(0, 16, 8):
            rows = pl.ds(first + sub, 8)
            pieces = []
            for x in range(2):
                for r in range(RA_DEV):
                    for hi in range(2):
                        rows_in = pl.ds(hi * half + first + sub, 8)
                        pieces.append(
                            sum_ref[r, x, rows_in, :] * inverse_ref[r, rows_in, :]
                        )
            pack_blocks(pieces, out_ref, rows)


def pack(summed, inverse):
    vmem = pl.BlockSpec(memory_space=pltpu.VMEM)
    return pl.pallas_call(
        pack_kernel,
        in_specs=[vmem, vmem],
        out_specs=vmem,
        out_shape=jax.ShapeDtypeStruct((N_BL, BASE_LOC // 2, 128), BF16),
        compiler_params=pltpu.CompilerParams(vmem_limit_bytes=16 * MIB),
        name="pack",
    )(summed, inverse)


def beam_kernel(block_ref, pair_ref, sep_ref, cos_ref, sin_ref, out_ref, grid_ref, table_buf):
    flat = BASES // 2
    rows = RA_DEV * PAIRS

    turned = block_ref[...].astype(F32).reshape(flat, 128).T
    total = jnp.zeros((2 * rows * BAND, NSEP), F32)
    for hi in range(2):
        picked = [
            turned[(group * 2 + hi) * BAND : (group * 2 + hi + 1) * BAND] for group in range(4)
        ]
        pair = pair_ref[hi : hi + 1, :]
        masked = jnp.concatenate(
            [jnp.where(pair == c, part, 0.0) for part in picked for c in range(PAIRS)], axis=0
        ).astype(BF16)
        sep = sep_ref[:, hi : hi + 1]
        column = jnp.where(
            sep >= NSEP // 2, sep - NSEP // 2, jnp.where(sep == 0, NSEP // 2, NSEP - sep)
        )
        onehot = jnp.where(
            column == lax.broadcasted_iota(jnp.int32, (flat, NSEP), 1), 1.0, 0.0
        ).astype(BF16)
        total = total + jnp.dot(masked, onehot, preferred_element_type=F32)
    for tile in range(NSEP // 128):
        grid_ref[tile] = total[:, tile * 128 : (tile + 1) * 128]

    flip = (
        lax.broadcasted_iota(jnp.int32, (HALF, HALF), 0)
        + lax.broadcasted_iota(jnp.int32, (HALF, HALF), 1)
        == HALF - 1
    )
    flip = jnp.where(flip, 1.0, 0.0).astype(BF16)
    odd_part = []
    edge = NSEP // 2 // FINE
    for f in range(BAND):
        cos_b = cos_ref[f, COARSE:, :]
        sin_b = sin_ref[f, COARSE:, :]
        for a in range(edge):
            cos_a = cos_ref[f, a : a + 1, :]
            sin_a = sin_ref[f, a : a + 1, :]
            at = pl.ds(a * FINE, FINE)
            table_buf[f, at, :HALF] = (cos_a * cos_b - sin_a * sin_b).astype(BF16)
            table_buf[f, at, HALF:] = (-(sin_a * cos_b + cos_a * sin_b)).astype(BF16)
        tiles = [grid_ref[tile, pl.ds(f, 2 * rows, stride=BAND), :] for tile in range(4)]
        cells = jnp.concatenate(
            [jnp.concatenate(tiles[:2], axis=1), jnp.concatenate(tiles[2:], axis=1)], axis=0
        ).astype(BF16)
        lone = tiles[2][:, :1]
        both = jnp.dot(cells, table_buf[f], preferred_element_type=F32)
        edge_cos = cos_ref[f, edge : edge + 1, :].astype(BF16).astype(F32)
        edge_sin = sin_ref[f, edge : edge + 1, :].astype(BF16).astype(F32)
        cos_part = both[:rows, :HALF] + both[2 * rows : 3 * rows, :HALF]
        cos_part = cos_part + lone[:rows] * (edge_cos - 1.0)
        sin_part = both[rows : 2 * rows, HALF:] - both[3 * rows :, HALF:]
        sin_part = sin_part + lone[rows:] * edge_sin
        even = cos_part + sin_part
        for r in range(RA_DEV):
            out_ref[f, r, :, :HALF] = even[r * PAIRS : (r + 1) * PAIRS]
        odd_part.append(cos_part - sin_part)
    rest = jnp.concatenate(odd_part, axis=0)
    turned = jnp.zeros(rest.shape, F32)
    for _ in range(3):
        piece = rest.astype(BF16)
        rest = rest - piece.astype(F32)
        turned = turned + jnp.dot(piece, flip, preferred_element_type=F32)
    for f in range(BAND):
        for r in range(RA_DEV):
            first = f * rows + r * PAIRS
            out_ref[f, r, :, HALF:] = turned[first : first + PAIRS]


def beam(block, pair_index, sep_index, angles):
    flat = BASES // 2
    pair = pair_index.reshape(N_BL, 2, BASE_LOC // 2).transpose(1, 0, 2).reshape(2, flat)
    sep = sep_index.reshape(N_BL, 2, BASE_LOC // 2).transpose(0, 2, 1).reshape(flat, 2)
    vmem = pl.BlockSpec(memory_space=pltpu.VMEM)
    return pl.pallas_call(
        beam_kernel,
        in_specs=[vmem] * 5,
        out_specs=vmem,
        out_shape=jax.ShapeDtypeStruct((BAND, RA_DEV, PAIRS, PIXELS), F32),
        scratch_shapes=[
            pltpu.VMEM((NSEP // 128, 2 * RA_DEV * PAIRS * BAND, 128), F32),
            pltpu.VMEM((BAND, NSEP // 2, 2 * HALF), BF16),
        ],
        compiler_params=pltpu.CompilerParams(vmem_limit_bytes=32 * MIB),
        name="beam",
    )(block, pair, sep, *angles)


def day_stage(visibility, day_weight, day_offset):
    visibility, day_weight = visibility[0], day_weight[0]
    other = lax.ppermute(select(day_offset, day_weight, visibility), "day", SWAP)
    weights = gather_weights(day_weight)
    sums = chip_sums(day_offset, visibility, day_weight, other)
    summed, weights = reduce_ring(sums, weights)
    return summed, inverse_total(day_offset, weights)


def beam_stage(summed, inverse, pair_index, sep_index, freq_at):
    packed = pack(summed, inverse)
    angles = base_angles(lax.optimization_barrier((freq_at, packed))[0])
    block = lax.all_to_all(packed, "bl", split_axis=0, concat_axis=0, tiled=True)
    return beam(block, pair_index, sep_index, angles)


def local(visibility, day_weight, day_offset, pair_index, sep_index):
    freq_at = (lax.axis_index("bl") * BAND + jnp.arange(BAND)).astype(F32)
    summed, inverse = day_stage(visibility, day_weight, day_offset)
    return beam_stage(summed, inverse, pair_index, sep_index, freq_at)


def solution(mesh):
    return jax.shard_map(
        local,
        mesh=mesh,
        in_specs=(P("day", None, None, "bl", None), P("day", "bl", None), P(), P(), P()),
        out_specs=P("bl", "day", None, None),
        check_vma=False,
    )
```

```python
import jax
import jax.numpy as jnp
from jax import lax
from jax.experimental import pallas as pl
from jax.experimental.pallas import tpu as pltpu
from jax.sharding import PartitionSpec as P

FREQ = 512
PAIRS = 4
NSEP = 512
PIXELS = 512
HALF = PIXELS // 2
RA = 32
RA_DEV = 2
SAMPLES = 16
DAYS = 16
BASES = 2048
N_BL = 32
BASE_LOC = BASES // N_BL
BAND = FREQ // N_BL
COARSE = 24
FINE = 16
CHIPS = 8
HELD = 8
SCALE = 128.0
SWAP = [(d, d ^ 1) for d in range(DAYS)]

F32 = jnp.float32
BF16 = jnp.bfloat16
F16 = jnp.float16
MIB = 1 << 20

phase_scale = 2.0 * 3.141592653589793 * 0.3048 / 299.792458


def bins_below(offset, core):
    return 2 * (offset >> 2) + jnp.clip((offset & 3) - 2 * core, 0, 2)


def select_kernel(offset_ref, weight_ref, vis_ref, out_ref, weight_buf, held_buf, sems):
    day = lax.axis_index("day")
    other = 1 - (day & 1)
    offset = offset_ref[day]
    first = bins_below(offset, other)
    load = pltpu.make_async_copy(weight_ref, weight_buf, sems.at[HELD])
    load.start()
    loads, stores = [], []
    for k in range(HELD):
        owned = first + k
        sample = 4 * (owned >> 1) + 2 * other + (owned & 1) - offset
        slot = owned & (HELD - 1)
        loads.append(pltpu.make_async_copy(vis_ref.at[sample], held_buf.at[k], sems.at[k]))
        loads[-1].start()
        stores.append(
            pltpu.make_async_copy(held_buf.at[k], out_ref.at[slot], sems.at[HELD + 1 + k])
        )
    load.wait()
    weight = weight_buf[...]
    high = weight.astype(BF16)
    held_buf[HELD, 0] = high
    held_buf[HELD, 1] = (weight - high.astype(F32)).astype(BF16)
    stores.append(
        pltpu.make_async_copy(held_buf.at[HELD], out_ref.at[HELD], sems.at[2 * HELD + 1])
    )
    stores[-1].start()
    for k in range(HELD):
        loads[k].wait()
        stores[k].start()
    for store in stores:
        store.wait()


def select(day_offset, day_weight, visibility):
    hbm = pl.BlockSpec(memory_space=pl.ANY)
    return pl.pallas_call(
        select_kernel,
        in_specs=[pl.BlockSpec(memory_space=pltpu.SMEM), hbm, hbm],
        out_specs=hbm,
        out_shape=jax.ShapeDtypeStruct((HELD + 1, 2, BASE_LOC, FREQ), BF16),
        scratch_shapes=[
            pltpu.VMEM((BASE_LOC, FREQ), F32),
            pltpu.VMEM((HELD + 1, 2, BASE_LOC, FREQ), BF16),
            pltpu.SemaphoreType.DMA((2 * HELD + 2,)),
        ],
        compiler_params=pltpu.CompilerParams(vmem_limit_bytes=60 * MIB),
        name="select",
    )(day_offset, day_weight, visibility)


SENDS = (
    ((3, 0), (3, 1), (1, 0), (1, 1)),
    ((5, 0), (5, 1), (7, 0), (7, 1)),
    ((4, 0),),
    ((4, 1),),
    ((2, 0), (2, 1)),
    ((6, 0), (6, 1)),
    ((0, 0), (0, 1)),
)


def chip_kernel(offset_ref, vis_ref, weight_ref, other_ref, *out_refs):
    day = lax.axis_index("day")
    core = day & 1
    chip = day >> 1
    offset = offset_ref[day]
    first = bins_below(offset_ref[day ^ 1], core)
    weight = weight_ref[...] * SCALE
    other_weight = (other_ref[HELD, 0].astype(F32) + other_ref[HELD, 1].astype(F32)) * SCALE
    for out_ref, bins in zip(out_refs, SENDS):
        for at, (distance, which) in enumerate(bins):
            owned = 2 * ((chip + distance) & (CHIPS - 1)) + which
            sample = 4 * (owned >> 1) + 2 * core + which - offset
            valid = jnp.logical_and(sample >= 0, sample < SAMPLES)
            held = jnp.logical_and(owned >= first, owned < first + HELD)
            sample = jnp.clip(sample, 0, SAMPLES - 1)
            own = weight * jnp.where(valid, 1.0, 0.0)
            other = other_weight * jnp.where(held, 1.0, 0.0)
            for x in range(2):
                out_ref[at, x] = (
                    vis_ref[sample, x].astype(F32) * own
                    + other_ref[owned & (HELD - 1), x].astype(F32) * other
                )


def chip_sums(day_offset, visibility, day_weight, other):
    rows = 16
    block = lambda count: pl.BlockSpec((count, 2, rows, FREQ), lambda i: (0, 0, i, 0))
    return pl.pallas_call(
        chip_kernel,
        grid=(BASE_LOC // rows,),
        in_specs=[
            pl.BlockSpec(memory_space=pltpu.SMEM),
            block(SAMPLES),
            pl.BlockSpec((rows, FREQ), lambda i: (i, 0)),
            block(HELD + 1),
        ],
        out_specs=[block(len(bins)) for bins in SENDS],
        out_shape=[
            jax.ShapeDtypeStruct((len(bins), 2, BASE_LOC, FREQ), F32) for bins in SENDS
        ],
        compiler_params=pltpu.CompilerParams(vmem_limit_bytes=16 * MIB),
        name="chip_sums",
    )(day_offset, visibility, day_weight, other)


def send(values, distance):
    pairs = [
        (2 * y + c, 2 * ((y + distance) % CHIPS) + c) for y in range(CHIPS) for c in range(2)
    ]
    return lax.ppermute(values, "day", pairs)


def reduce_ring(sums, late):
    first = lax.optimization_barrier([part.astype(F16) for part in sums[:4]])
    near_up, near_down = send(first[0], 1), send(first[1], -1)
    far_up, far_down = send(first[2], 2), send(first[3], -2)
    middle_up = sums[4] + near_up[:2].astype(F32)
    middle_up = middle_up + jnp.pad(far_up.astype(F32), ((0, 1), (0, 0), (0, 0), (0, 0)))
    middle_down = sums[5] + near_down[:2].astype(F32)
    middle_down = middle_down + jnp.pad(far_down.astype(F32), ((1, 0), (0, 0), (0, 0), (0, 0)))
    middle_up, middle_down = middle_up.astype(F16), middle_down.astype(F16)
    last_up, last_down = send(middle_up, 2), send(middle_down, -2)
    late = lax.optimization_barrier((late, last_up))[0]
    summed = (
        sums[6]
        + near_up[2:].astype(F32)
        + near_down[2:].astype(F32)
        + last_up.astype(F32)
        + last_down.astype(F32)
    )
    return summed, late


def gather_weights(day_weight):
    same = [[2 * y + c for y in range(CHIPS)] for c in range(2)]
    copies = jnp.broadcast_to(day_weight.astype(F16)[None], (CHIPS, BASE_LOC, FREQ))
    return lax.all_to_all(
        copies, "day", split_axis=0, concat_axis=0, axis_index_groups=same, tiled=True
    )


def inverse_total(day_offset, weights):
    day = lax.axis_index("day")
    offsets = jnp.where((day & 1) == 0, day_offset[0::2], day_offset[1::2])
    at = jnp.arange(2 * RA_DEV)
    bins = (day ^ (at // RA_DEV)) * RA_DEV + at % RA_DEV
    sample = bins[:, None] - offsets[None, :]
    valid = jnp.logical_and(sample >= 0, sample < SAMPLES).astype(F32)
    totals = jnp.sum(valid[:, :, None, None] * weights[None].astype(F32), axis=1)
    other = lax.ppermute(totals[RA_DEV:], "day", SWAP)
    return (1.0 / SCALE) / (totals[:RA_DEV] + other)


def base_angles(freq_at):
    factor = phase_scale * (800.0 - 400.0 * (freq_at + 0.5) / FREQ)
    sine_dir = -1.0 + 2.0 * (jnp.arange(HALF).astype(F32) + 0.5) / PIXELS
    separation = jnp.concatenate([jnp.arange(COARSE) * FINE, jnp.arange(FINE)]).astype(F32)
    phase = factor[:, None, None] * separation[None, :, None] * sine_dir[None, None, :]
    return jnp.cos(phase), jnp.sin(phase)


def pack_blocks(pieces, out_ref, rows):
    lane_group = lax.broadcasted_iota(jnp.int32, (8, 128), 1) // BAND
    for tile in range(FREQ // 128):
        parts = [piece[:, tile * 128 : (tile + 1) * 128] for piece in pieces]
        for step in (4, 2, 1):
            keep = (lane_group & step) == 0
            mixed = list(parts)
            for low in range(8):
                if low & step:
                    continue
                high = low | step
                mixed[low] = jnp.where(keep, parts[low], pltpu.roll(parts[high], step * BAND, 1))
                mixed[high] = jnp.where(
                    keep, pltpu.roll(parts[low], 128 - step * BAND, 1), parts[high]
                )
            parts = mixed
        for group in range(8):
            out_ref[tile * 8 + group, rows, :] = parts[group].astype(BF16)


def pack_kernel(sum_ref, inverse_ref, out_ref):
    half = BASE_LOC // 2
    for first in range(0, half, 16):
        for sub in range(0, 16, 8):
            rows = pl.ds(first + sub, 8)
            pieces = []
            for x in range(2):
                for r in range(RA_DEV):
                    for hi in range(2):
                        rows_in = pl.ds(hi * half + first + sub, 8)
                        pieces.append(
                            sum_ref[r, x, rows_in, :] * inverse_ref[r, rows_in, :]
                        )
            pack_blocks(pieces, out_ref, rows)


def pack(summed, inverse):
    vmem = pl.BlockSpec(memory_space=pltpu.VMEM)
    return pl.pallas_call(
        pack_kernel,
        in_specs=[vmem, vmem],
        out_specs=vmem,
        out_shape=jax.ShapeDtypeStruct((N_BL, BASE_LOC // 2, 128), BF16),
        compiler_params=pltpu.CompilerParams(vmem_limit_bytes=16 * MIB),
        name="pack",
    )(summed, inverse)


def beam_kernel(block_ref, pair_ref, sep_ref, cos_ref, sin_ref, out_ref, grid_ref, table_buf):
    flat = BASES // 2
    rows = RA_DEV * PAIRS

    turned = block_ref[...].astype(F32).reshape(flat, 128).T
    total = jnp.zeros((2 * rows * BAND, NSEP), F32)
    for hi in range(2):
        picked = [
            turned[(group * 2 + hi) * BAND : (group * 2 + hi + 1) * BAND] for group in range(4)
        ]
        pair = pair_ref[hi : hi + 1, :]
        masked = jnp.concatenate(
            [jnp.where(pair == c, part, 0.0) for part in picked for c in range(PAIRS)], axis=0
        ).astype(BF16)
        sep = sep_ref[:, hi : hi + 1]
        column = jnp.where(
            sep >= NSEP // 2, sep - NSEP // 2, jnp.where(sep == 0, NSEP // 2, NSEP - sep)
        )
        onehot = jnp.where(
            column == lax.broadcasted_iota(jnp.int32, (flat, NSEP), 1), 1.0, 0.0
        ).astype(BF16)
        total = total + jnp.dot(masked, onehot, preferred_element_type=F32)
    for tile in range(NSEP // 128):
        grid_ref[tile] = total[:, tile * 128 : (tile + 1) * 128]

    flip = (
        lax.broadcasted_iota(jnp.int32, (HALF, HALF), 0)
        + lax.broadcasted_iota(jnp.int32, (HALF, HALF), 1)
        == HALF - 1
    )
    flip = jnp.where(flip, 1.0, 0.0).astype(BF16)
    odd_part = []
    edge = NSEP // 2 // FINE
    for f in range(BAND):
        cos_b = cos_ref[f, COARSE:, :]
        sin_b = sin_ref[f, COARSE:, :]
        for a in range(edge):
            cos_a = cos_ref[f, a : a + 1, :]
            sin_a = sin_ref[f, a : a + 1, :]
            at = pl.ds(a * FINE, FINE)
            table_buf[f, at, :HALF] = (cos_a * cos_b - sin_a * sin_b).astype(BF16)
            table_buf[f, at, HALF:] = (-(sin_a * cos_b + cos_a * sin_b)).astype(BF16)
        tiles = [grid_ref[tile, pl.ds(f, 2 * rows, stride=BAND), :] for tile in range(4)]
        cells = jnp.concatenate(
            [jnp.concatenate(tiles[:2], axis=1), jnp.concatenate(tiles[2:], axis=1)], axis=0
        ).astype(BF16)
        lone = tiles[2][:, :1]
        both = jnp.dot(cells, table_buf[f], preferred_element_type=F32)
        edge_cos = cos_ref[f, edge : edge + 1, :].astype(BF16).astype(F32)
        edge_sin = sin_ref[f, edge : edge + 1, :].astype(BF16).astype(F32)
        cos_part = both[:rows, :HALF] + both[2 * rows : 3 * rows, :HALF]
        cos_part = cos_part + lone[:rows] * (edge_cos - 1.0)
        sin_part = both[rows : 2 * rows, HALF:] - both[3 * rows :, HALF:]
        sin_part = sin_part + lone[rows:] * edge_sin
        even = cos_part + sin_part
        for r in range(RA_DEV):
            out_ref[f, r, :, :HALF] = even[r * PAIRS : (r + 1) * PAIRS]
        odd_part.append(cos_part - sin_part)
    rest = jnp.concatenate(odd_part, axis=0)
    turned = jnp.zeros(rest.shape, F32)
    for _ in range(3):
        piece = rest.astype(BF16)
        rest = rest - piece.astype(F32)
        turned = turned + jnp.dot(piece, flip, preferred_element_type=F32)
    for f in range(BAND):
        for r in range(RA_DEV):
            first = f * rows + r * PAIRS
            out_ref[f, r, :, HALF:] = turned[first : first + PAIRS]


def beam(block, pair_index, sep_index, angles):
    flat = BASES // 2
    pair = pair_index.reshape(N_BL, 2, BASE_LOC // 2).transpose(1, 0, 2).reshape(2, flat)
    sep = sep_index.reshape(N_BL, 2, BASE_LOC // 2).transpose(0, 2, 1).reshape(flat, 2)
    vmem = pl.BlockSpec(memory_space=pltpu.VMEM)
    return pl.pallas_call(
        beam_kernel,
        in_specs=[vmem] * 5,
        out_specs=vmem,
        out_shape=jax.ShapeDtypeStruct((BAND, RA_DEV, PAIRS, PIXELS), F32),
        scratch_shapes=[
            pltpu.VMEM((NSEP // 128, 2 * RA_DEV * PAIRS * BAND, 128), F32),
            pltpu.VMEM((BAND, NSEP // 2, 2 * HALF), BF16),
        ],
        compiler_params=pltpu.CompilerParams(vmem_limit_bytes=32 * MIB),
        name="beam",
    )(block, pair, sep, *angles)


def day_stage(visibility, day_weight, day_offset):
    visibility, day_weight = visibility[0], day_weight[0]
    other = lax.ppermute(select(day_offset, day_weight, visibility), "day", SWAP)
    weights = gather_weights(day_weight)
    sums = chip_sums(day_offset, visibility, day_weight, other)
    summed, weights = reduce_ring(sums, weights)
    return summed, inverse_total(day_offset, weights)


def beam_stage(summed, inverse, pair_index, sep_index):
    freq_at = (lax.axis_index("bl") * BAND + jnp.arange(BAND)).astype(F32)
    packed = pack(summed, inverse)
    pair_index, sep_index, freq_at, _ = lax.optimization_barrier(
        (pair_index, sep_index, freq_at, packed)
    )
    angles = base_angles(freq_at)
    block = lax.all_to_all(packed, "bl", split_axis=0, concat_axis=0, tiled=True)
    return beam(block, pair_index, sep_index, angles)


def local(visibility, day_weight, day_offset, pair_index, sep_index):
    summed, inverse = day_stage(visibility, day_weight, day_offset)
    return beam_stage(summed, inverse, pair_index, sep_index)


def solution(mesh):
    return jax.shard_map(
        local,
        mesh=mesh,
        in_specs=(P("day", None, None, "bl", None), P("day", "bl", None), P(), P(), P()),
        out_specs=P("bl", "day", None, None),
        check_vma=False,
    )
```

```python
import jax
import jax.numpy as jnp
from jax import lax
from jax.experimental import pallas as pl
from jax.experimental.pallas import tpu as pltpu
from jax.sharding import PartitionSpec as P

FREQ = 512
PAIRS = 4
NSEP = 512
PIXELS = 512
HALF = PIXELS // 2
RA = 32
RA_DEV = 2
SAMPLES = 16
DAYS = 16
BASES = 2048
N_BL = 32
BASE_LOC = BASES // N_BL
BAND = FREQ // N_BL
COARSE = 24
FINE = 16
CHIPS = 8
HELD = 8
SCALE = 128.0
SWAP = [(d, d ^ 1) for d in range(DAYS)]

F32 = jnp.float32
BF16 = jnp.bfloat16
F16 = jnp.float16
MIB = 1 << 20

phase_scale = 2.0 * 3.141592653589793 * 0.3048 / 299.792458


def bins_below(offset, core):
    return 2 * (offset >> 2) + jnp.clip((offset & 3) - 2 * core, 0, 2)


def select_kernel(offset_ref, weight_ref, vis_ref, out_ref, weight_buf, held_buf, sems):
    day = lax.axis_index("day")
    other = 1 - (day & 1)
    offset = offset_ref[day]
    first = bins_below(offset, other)
    load = pltpu.make_async_copy(weight_ref, weight_buf, sems.at[HELD])
    load.start()
    loads, stores = [], []
    for k in range(HELD):
        owned = first + k
        sample = 4 * (owned >> 1) + 2 * other + (owned & 1) - offset
        slot = owned & (HELD - 1)
        loads.append(pltpu.make_async_copy(vis_ref.at[sample], held_buf.at[k], sems.at[k]))
        loads[-1].start()
        stores.append(
            pltpu.make_async_copy(held_buf.at[k], out_ref.at[slot], sems.at[HELD + 1 + k])
        )
    load.wait()
    weight = weight_buf[...]
    high = weight.astype(BF16)
    held_buf[HELD, 0] = high
    held_buf[HELD, 1] = (weight - high.astype(F32)).astype(BF16)
    stores.append(
        pltpu.make_async_copy(held_buf.at[HELD], out_ref.at[HELD], sems.at[2 * HELD + 1])
    )
    stores[-1].start()
    for k in range(HELD):
        loads[k].wait()
        stores[k].start()
    for store in stores:
        store.wait()


def select(day_offset, day_weight, visibility):
    hbm = pl.BlockSpec(memory_space=pl.ANY)
    return pl.pallas_call(
        select_kernel,
        in_specs=[pl.BlockSpec(memory_space=pltpu.SMEM), hbm, hbm],
        out_specs=hbm,
        out_shape=jax.ShapeDtypeStruct((HELD + 1, 2, BASE_LOC, FREQ), BF16),
        scratch_shapes=[
            pltpu.VMEM((BASE_LOC, FREQ), F32),
            pltpu.VMEM((HELD + 1, 2, BASE_LOC, FREQ), BF16),
            pltpu.SemaphoreType.DMA((2 * HELD + 2,)),
        ],
        compiler_params=pltpu.CompilerParams(vmem_limit_bytes=60 * MIB),
        name="select",
    )(day_offset, day_weight, visibility)


SENDS = (
    ((3, 0), (3, 1), (1, 0), (1, 1)),
    ((5, 0), (5, 1), (7, 0), (7, 1)),
    ((4, 0),),
    ((4, 1),),
    ((2, 0), (2, 1)),
    ((6, 0), (6, 1)),
    ((0, 0), (0, 1)),
)


def chip_kernel(offset_ref, vis_ref, weight_ref, other_ref, *out_refs):
    day = lax.axis_index("day")
    core = day & 1
    chip = day >> 1
    offset = offset_ref[day]
    first = bins_below(offset_ref[day ^ 1], core)
    weight = weight_ref[...] * SCALE
    other_weight = (other_ref[HELD, 0].astype(F32) + other_ref[HELD, 1].astype(F32)) * SCALE
    for out_ref, bins in zip(out_refs, SENDS):
        for at, (distance, which) in enumerate(bins):
            owned = 2 * ((chip + distance) & (CHIPS - 1)) + which
            sample = 4 * (owned >> 1) + 2 * core + which - offset
            valid = jnp.logical_and(sample >= 0, sample < SAMPLES)
            held = jnp.logical_and(owned >= first, owned < first + HELD)
            sample = jnp.clip(sample, 0, SAMPLES - 1)
            own = weight * jnp.where(valid, 1.0, 0.0)
            other = other_weight * jnp.where(held, 1.0, 0.0)
            for x in range(2):
                out_ref[at, x] = (
                    vis_ref[sample, x].astype(F32) * own
                    + other_ref[owned & (HELD - 1), x].astype(F32) * other
                )


def chip_sums(day_offset, visibility, day_weight, other):
    rows = 16
    block = lambda count: pl.BlockSpec((count, 2, rows, FREQ), lambda i: (0, 0, i, 0))
    return pl.pallas_call(
        chip_kernel,
        grid=(BASE_LOC // rows,),
        in_specs=[
            pl.BlockSpec(memory_space=pltpu.SMEM),
            block(SAMPLES),
            pl.BlockSpec((rows, FREQ), lambda i: (i, 0)),
            block(HELD + 1),
        ],
        out_specs=[block(len(bins)) for bins in SENDS],
        out_shape=[
            jax.ShapeDtypeStruct((len(bins), 2, BASE_LOC, FREQ), F32) for bins in SENDS
        ],
        compiler_params=pltpu.CompilerParams(vmem_limit_bytes=16 * MIB),
        name="chip_sums",
    )(day_offset, visibility, day_weight, other)


def send(values, distance):
    pairs = [
        (2 * y + c, 2 * ((y + distance) % CHIPS) + c) for y in range(CHIPS) for c in range(2)
    ]
    return lax.ppermute(values, "day", pairs)


def reduce_ring(sums, late):
    first = lax.optimization_barrier([part.astype(F16) for part in sums[:4]])
    near_up, near_down = send(first[0], 1), send(first[1], -1)
    far_up, far_down = send(first[2], 2), send(first[3], -2)
    middle_up = sums[4] + near_up[:2].astype(F32)
    middle_up = middle_up + jnp.pad(far_up.astype(F32), ((0, 1), (0, 0), (0, 0), (0, 0)))
    middle_down = sums[5] + near_down[:2].astype(F32)
    middle_down = middle_down + jnp.pad(far_down.astype(F32), ((1, 0), (0, 0), (0, 0), (0, 0)))
    middle_up, middle_down = middle_up.astype(F16), middle_down.astype(F16)
    last_up, last_down = send(middle_up, 2), send(middle_down, -2)
    late = lax.optimization_barrier((late, last_up))[0]
    summed = (
        sums[6]
        + near_up[2:].astype(F32)
        + near_down[2:].astype(F32)
        + last_up.astype(F32)
        + last_down.astype(F32)
    )
    return summed, late


def gather_weights(day_weight):
    same = [[2 * y + c for y in range(CHIPS)] for c in range(2)]
    return lax.all_gather(day_weight.astype(F16), "day", axis=0, axis_index_groups=same)


def inverse_total(day_offset, weights):
    day = lax.axis_index("day")
    offsets = jnp.where((day & 1) == 0, day_offset[0::2], day_offset[1::2])
    at = jnp.arange(2 * RA_DEV)
    bins = (day ^ (at // RA_DEV)) * RA_DEV + at % RA_DEV
    sample = bins[:, None] - offsets[None, :]
    valid = jnp.logical_and(sample >= 0, sample < SAMPLES).astype(F32)
    totals = jnp.sum(valid[:, :, None, None] * weights[None].astype(F32), axis=1)
    other = lax.ppermute(totals[RA_DEV:], "day", SWAP)
    return (1.0 / SCALE) / (totals[:RA_DEV] + other)


def base_angles(freq_at):
    factor = phase_scale * (800.0 - 400.0 * (freq_at + 0.5) / FREQ)
    sine_dir = -1.0 + 2.0 * (jnp.arange(HALF).astype(F32) + 0.5) / PIXELS
    separation = jnp.concatenate([jnp.arange(COARSE) * FINE, jnp.arange(FINE)]).astype(F32)
    phase = factor[:, None, None] * separation[None, :, None] * sine_dir[None, None, :]
    return jnp.cos(phase), jnp.sin(phase)


def pack_blocks(pieces, out_ref, rows):
    lane_group = lax.broadcasted_iota(jnp.int32, (8, 128), 1) // BAND
    for tile in range(FREQ // 128):
        parts = [piece[:, tile * 128 : (tile + 1) * 128] for piece in pieces]
        for step in (4, 2, 1):
            keep = (lane_group & step) == 0
            mixed = list(parts)
            for low in range(8):
                if low & step:
                    continue
                high = low | step
                mixed[low] = jnp.where(keep, parts[low], pltpu.roll(parts[high], step * BAND, 1))
                mixed[high] = jnp.where(
                    keep, pltpu.roll(parts[low], 128 - step * BAND, 1), parts[high]
                )
            parts = mixed
        for group in range(8):
            out_ref[tile * 8 + group, rows, :] = parts[group].astype(BF16)


def pack_kernel(sum_ref, inverse_ref, out_ref):
    half = BASE_LOC // 2
    for first in range(0, half, 16):
        for sub in range(0, 16, 8):
            rows = pl.ds(first + sub, 8)
            pieces = []
            for x in range(2):
                for r in range(RA_DEV):
                    for hi in range(2):
                        rows_in = pl.ds(hi * half + first + sub, 8)
                        pieces.append(
                            sum_ref[r, x, rows_in, :] * inverse_ref[r, rows_in, :]
                        )
            pack_blocks(pieces, out_ref, rows)


def pack(summed, inverse):
    vmem = pl.BlockSpec(memory_space=pltpu.VMEM)
    return pl.pallas_call(
        pack_kernel,
        in_specs=[vmem, vmem],
        out_specs=vmem,
        out_shape=jax.ShapeDtypeStruct((N_BL, BASE_LOC // 2, 128), BF16),
        compiler_params=pltpu.CompilerParams(vmem_limit_bytes=16 * MIB),
        name="pack",
    )(summed, inverse)


def beam_kernel(block_ref, pair_ref, sep_ref, cos_ref, sin_ref, out_ref, grid_ref, table_buf):
    flat = BASES // 2
    rows = RA_DEV * PAIRS

    turned = block_ref[...].astype(F32).reshape(flat, 128).T
    total = jnp.zeros((2 * rows * BAND, NSEP), F32)
    for hi in range(2):
        picked = [
            turned[(group * 2 + hi) * BAND : (group * 2 + hi + 1) * BAND] for group in range(4)
        ]
        pair = pair_ref[hi : hi + 1, :]
        masked = jnp.concatenate(
            [jnp.where(pair == c, part, 0.0) for part in picked for c in range(PAIRS)], axis=0
        ).astype(BF16)
        sep = sep_ref[:, hi : hi + 1]
        column = jnp.where(
            sep >= NSEP // 2, sep - NSEP // 2, jnp.where(sep == 0, NSEP // 2, NSEP - sep)
        )
        onehot = jnp.where(
            column == lax.broadcasted_iota(jnp.int32, (flat, NSEP), 1), 1.0, 0.0
        ).astype(BF16)
        total = total + jnp.dot(masked, onehot, preferred_element_type=F32)
    for tile in range(NSEP // 128):
        grid_ref[tile] = total[:, tile * 128 : (tile + 1) * 128]

    flip = (
        lax.broadcasted_iota(jnp.int32, (HALF, HALF), 0)
        + lax.broadcasted_iota(jnp.int32, (HALF, HALF), 1)
        == HALF - 1
    )
    flip = jnp.where(flip, 1.0, 0.0).astype(BF16)
    odd_part = []
    edge = NSEP // 2 // FINE
    for f in range(BAND):
        cos_b = cos_ref[f, COARSE:, :]
        sin_b = sin_ref[f, COARSE:, :]
        for a in range(edge):
            cos_a = cos_ref[f, a : a + 1, :]
            sin_a = sin_ref[f, a : a + 1, :]
            at = pl.ds(a * FINE, FINE)
            table_buf[f, at, :HALF] = (cos_a * cos_b - sin_a * sin_b).astype(BF16)
            table_buf[f, at, HALF:] = (-(sin_a * cos_b + cos_a * sin_b)).astype(BF16)
        tiles = [grid_ref[tile, pl.ds(f, 2 * rows, stride=BAND), :] for tile in range(4)]
        cells = jnp.concatenate(
            [jnp.concatenate(tiles[:2], axis=1), jnp.concatenate(tiles[2:], axis=1)], axis=0
        ).astype(BF16)
        lone = tiles[2][:, :1]
        both = jnp.dot(cells, table_buf[f], preferred_element_type=F32)
        edge_cos = cos_ref[f, edge : edge + 1, :].astype(BF16).astype(F32)
        edge_sin = sin_ref[f, edge : edge + 1, :].astype(BF16).astype(F32)
        cos_part = both[:rows, :HALF] + both[2 * rows : 3 * rows, :HALF]
        cos_part = cos_part + lone[:rows] * (edge_cos - 1.0)
        sin_part = both[rows : 2 * rows, HALF:] - both[3 * rows :, HALF:]
        sin_part = sin_part + lone[rows:] * edge_sin
        even = cos_part + sin_part
        for r in range(RA_DEV):
            out_ref[f, r, :, :HALF] = even[r * PAIRS : (r + 1) * PAIRS]
        odd_part.append(cos_part - sin_part)
    rest = jnp.concatenate(odd_part, axis=0)
    turned = jnp.zeros(rest.shape, F32)
    for _ in range(3):
        piece = rest.astype(BF16)
        rest = rest - piece.astype(F32)
        turned = turned + jnp.dot(piece, flip, preferred_element_type=F32)
    for f in range(BAND):
        for r in range(RA_DEV):
            first = f * rows + r * PAIRS
            out_ref[f, r, :, HALF:] = turned[first : first + PAIRS]


def beam(block, pair_index, sep_index, angles):
    flat = BASES // 2
    pair = pair_index.reshape(N_BL, 2, BASE_LOC // 2).transpose(1, 0, 2).reshape(2, flat)
    sep = sep_index.reshape(N_BL, 2, BASE_LOC // 2).transpose(0, 2, 1).reshape(flat, 2)
    vmem = pl.BlockSpec(memory_space=pltpu.VMEM)
    return pl.pallas_call(
        beam_kernel,
        in_specs=[vmem] * 5,
        out_specs=vmem,
        out_shape=jax.ShapeDtypeStruct((BAND, RA_DEV, PAIRS, PIXELS), F32),
        scratch_shapes=[
            pltpu.VMEM((NSEP // 128, 2 * RA_DEV * PAIRS * BAND, 128), F32),
            pltpu.VMEM((BAND, NSEP // 2, 2 * HALF), BF16),
        ],
        compiler_params=pltpu.CompilerParams(vmem_limit_bytes=32 * MIB),
        name="beam",
    )(block, pair, sep, *angles)


def day_stage(visibility, day_weight, day_offset):
    visibility, day_weight = visibility[0], day_weight[0]
    other = lax.ppermute(select(day_offset, day_weight, visibility), "day", SWAP)
    other, weights = lax.optimization_barrier((other, gather_weights(day_weight)))
    sums = chip_sums(day_offset, visibility, day_weight, other)
    summed, weights = reduce_ring(sums, weights)
    return summed, inverse_total(day_offset, weights)


def beam_stage(summed, inverse, pair_index, sep_index):
    freq_at = (lax.axis_index("bl") * BAND + jnp.arange(BAND)).astype(F32)
    packed = pack(summed, inverse)
    pair_index, sep_index, freq_at, _ = lax.optimization_barrier(
        (pair_index, sep_index, freq_at, packed)
    )
    angles = base_angles(freq_at)
    block = lax.all_to_all(packed, "bl", split_axis=0, concat_axis=0, tiled=True)
    return beam(block, pair_index, sep_index, angles)


def local(visibility, day_weight, day_offset, pair_index, sep_index):
    summed, inverse = day_stage(visibility, day_weight, day_offset)
    return beam_stage(summed, inverse, pair_index, sep_index)


def solution(mesh):
    return jax.shard_map(
        local,
        mesh=mesh,
        in_specs=(P("day", None, None, "bl", None), P("day", "bl", None), P(), P(), P()),
        out_specs=P("bl", "day", None, None),
        check_vma=False,
    )
```

```python
import jax
import jax.numpy as jnp
from jax import lax
from jax.experimental import pallas as pl
from jax.experimental.pallas import tpu as pltpu
from jax.sharding import PartitionSpec as P

FREQ = 512
PAIRS = 4
NSEP = 512
PIXELS = 512
HALF = PIXELS // 2
RA = 32
RA_DEV = 2
SAMPLES = 16
DAYS = 16
BASES = 2048
N_BL = 32
BASE_LOC = BASES // N_BL
BAND = FREQ // N_BL
COARSE = 24
FINE = 16
CHIPS = 8
HELD = 8
SCALE = 128.0
SWAP = [(d, d ^ 1) for d in range(DAYS)]

F32 = jnp.float32
BF16 = jnp.bfloat16
F16 = jnp.float16
MIB = 1 << 20

phase_scale = 2.0 * 3.141592653589793 * 0.3048 / 299.792458


def bins_below(offset, core):
    return 2 * (offset >> 2) + jnp.clip((offset & 3) - 2 * core, 0, 2)


def select_kernel(offset_ref, weight_ref, vis_ref, out_ref, weight_buf, held_buf, sems):
    day = lax.axis_index("day")
    other = 1 - (day & 1)
    offset = offset_ref[day]
    first = bins_below(offset, other)
    load = pltpu.make_async_copy(weight_ref, weight_buf, sems.at[HELD])
    load.start()
    loads, stores = [], []
    for k in range(HELD):
        owned = first + k
        sample = 4 * (owned >> 1) + 2 * other + (owned & 1) - offset
        slot = owned & (HELD - 1)
        loads.append(pltpu.make_async_copy(vis_ref.at[sample], held_buf.at[k], sems.at[k]))
        loads[-1].start()
        stores.append(
            pltpu.make_async_copy(held_buf.at[k], out_ref.at[slot], sems.at[HELD + 1 + k])
        )
    load.wait()
    weight = weight_buf[...]
    high = weight.astype(BF16)
    held_buf[HELD, 0] = high
    held_buf[HELD, 1] = (weight - high.astype(F32)).astype(BF16)
    stores.append(
        pltpu.make_async_copy(held_buf.at[HELD], out_ref.at[HELD], sems.at[2 * HELD + 1])
    )
    stores[-1].start()
    for k in range(HELD):
        loads[k].wait()
        stores[k].start()
    for store in stores:
        store.wait()


def select(day_offset, day_weight, visibility):
    hbm = pl.BlockSpec(memory_space=pl.ANY)
    return pl.pallas_call(
        select_kernel,
        in_specs=[pl.BlockSpec(memory_space=pltpu.SMEM), hbm, hbm],
        out_specs=hbm,
        out_shape=jax.ShapeDtypeStruct((HELD + 1, 2, BASE_LOC, FREQ), BF16),
        scratch_shapes=[
            pltpu.VMEM((BASE_LOC, FREQ), F32),
            pltpu.VMEM((HELD + 1, 2, BASE_LOC, FREQ), BF16),
            pltpu.SemaphoreType.DMA((2 * HELD + 2,)),
        ],
        compiler_params=pltpu.CompilerParams(vmem_limit_bytes=60 * MIB),
        name="select",
    )(day_offset, day_weight, visibility)


SENDS = (
    ((3, 0), (3, 1), (1, 0), (1, 1)),
    ((5, 0), (5, 1), (7, 0), (7, 1)),
    ((4, 0),),
    ((4, 1),),
    ((2, 0), (2, 1)),
    ((6, 0), (6, 1)),
    ((0, 0), (0, 1)),
)


def chip_kernel(offset_ref, vis_ref, weight_ref, other_ref, *out_refs):
    day = lax.axis_index("day")
    core = day & 1
    chip = day >> 1
    offset = offset_ref[day]
    first = bins_below(offset_ref[day ^ 1], core)
    weight = weight_ref[...] * SCALE
    other_weight = (other_ref[HELD, 0].astype(F32) + other_ref[HELD, 1].astype(F32)) * SCALE
    for out_ref, bins in zip(out_refs, SENDS):
        for at, (distance, which) in enumerate(bins):
            owned = 2 * ((chip + distance) & (CHIPS - 1)) + which
            sample = 4 * (owned >> 1) + 2 * core + which - offset
            valid = jnp.logical_and(sample >= 0, sample < SAMPLES)
            held = jnp.logical_and(owned >= first, owned < first + HELD)
            sample = jnp.clip(sample, 0, SAMPLES - 1)
            own = weight * jnp.where(valid, 1.0, 0.0)
            other = other_weight * jnp.where(held, 1.0, 0.0)
            for x in range(2):
                out_ref[at, x] = (
                    vis_ref[sample, x].astype(F32) * own
                    + other_ref[owned & (HELD - 1), x].astype(F32) * other
                )
            out_ref[at, 2] = own + other


def chip_sums(day_offset, visibility, day_weight, other):
    rows = 16
    block = lambda count, parts: pl.BlockSpec((count, parts, rows, FREQ), lambda i: (0, 0, i, 0))
    return pl.pallas_call(
        chip_kernel,
        grid=(BASE_LOC // rows,),
        in_specs=[
            pl.BlockSpec(memory_space=pltpu.SMEM),
            block(SAMPLES, 2),
            pl.BlockSpec((rows, FREQ), lambda i: (i, 0)),
            block(HELD + 1, 2),
        ],
        out_specs=[block(len(bins), 3) for bins in SENDS],
        out_shape=[
            jax.ShapeDtypeStruct((len(bins), 3, BASE_LOC, FREQ), F32) for bins in SENDS
        ],
        compiler_params=pltpu.CompilerParams(vmem_limit_bytes=16 * MIB),
        name="chip_sums",
    )(day_offset, visibility, day_weight, other)


def send(values, distance):
    pairs = [
        (2 * y + c, 2 * ((y + distance) % CHIPS) + c) for y in range(CHIPS) for c in range(2)
    ]
    return lax.ppermute(values, "day", pairs)


def reduce_ring(sums):
    first = lax.optimization_barrier([part.astype(F16) for part in sums[:4]])
    near_up, near_down = send(first[0], 1), send(first[1], -1)
    far_up, far_down = send(first[2], 2), send(first[3], -2)
    middle_up = sums[4] + near_up[:2].astype(F32)
    middle_up = middle_up + jnp.pad(far_up.astype(F32), ((0, 1), (0, 0), (0, 0), (0, 0)))
    middle_down = sums[5] + near_down[:2].astype(F32)
    middle_down = middle_down + jnp.pad(far_down.astype(F32), ((1, 0), (0, 0), (0, 0), (0, 0)))
    middle_up, middle_down = middle_up.astype(F16), middle_down.astype(F16)
    last_up, last_down = send(middle_up, 2), send(middle_down, -2)
    return (
        sums[6]
        + near_up[2:].astype(F32)
        + near_down[2:].astype(F32)
        + last_up.astype(F32)
        + last_down.astype(F32)
    )


def base_angles(freq_at):
    factor = phase_scale * (800.0 - 400.0 * (freq_at + 0.5) / FREQ)
    sine_dir = -1.0 + 2.0 * (jnp.arange(HALF).astype(F32) + 0.5) / PIXELS
    separation = jnp.concatenate([jnp.arange(COARSE) * FINE, jnp.arange(FINE)]).astype(F32)
    phase = factor[:, None, None] * separation[None, :, None] * sine_dir[None, None, :]
    return jnp.cos(phase), jnp.sin(phase)


def pack_blocks(pieces, out_ref, rows):
    lane_group = lax.broadcasted_iota(jnp.int32, (8, 128), 1) // BAND
    for tile in range(FREQ // 128):
        parts = [piece[:, tile * 128 : (tile + 1) * 128] for piece in pieces]
        for step in (4, 2, 1):
            keep = (lane_group & step) == 0
            mixed = list(parts)
            for low in range(8):
                if low & step:
                    continue
                high = low | step
                mixed[low] = jnp.where(keep, parts[low], pltpu.roll(parts[high], step * BAND, 1))
                mixed[high] = jnp.where(
                    keep, pltpu.roll(parts[low], 128 - step * BAND, 1), parts[high]
                )
            parts = mixed
        for group in range(8):
            out_ref[tile * 8 + group, rows, :] = parts[group].astype(BF16)


def pack_kernel(sum_ref, out_ref):
    half = BASE_LOC // 2
    for first in range(0, half, 16):
        for sub in range(0, 16, 8):
            rows = pl.ds(first + sub, 8)
            pieces = [None] * 8
            for r in range(RA_DEV):
                for hi in range(2):
                    rows_in = pl.ds(hi * half + first + sub, 8)
                    inverse = 1.0 / sum_ref[r, 2, rows_in, :]
                    for x in range(2):
                        pieces[x * 4 + r * 2 + hi] = sum_ref[r, x, rows_in, :] * inverse
            pack_blocks(pieces, out_ref, rows)


def pack(summed):
    vmem = pl.BlockSpec(memory_space=pltpu.VMEM)
    return pl.pallas_call(
        pack_kernel,
        in_specs=[vmem],
        out_specs=vmem,
        out_shape=jax.ShapeDtypeStruct((N_BL, BASE_LOC // 2, 128), BF16),
        compiler_params=pltpu.CompilerParams(vmem_limit_bytes=16 * MIB),
        name="pack",
    )(summed)


def beam_kernel(block_ref, pair_ref, sep_ref, cos_ref, sin_ref, out_ref, grid_ref, table_buf):
    flat = BASES // 2
    rows = RA_DEV * PAIRS

    turned = block_ref[...].astype(F32).reshape(flat, 128).T
    total = jnp.zeros((2 * rows * BAND, NSEP), F32)
    for hi in range(2):
        picked = [
            turned[(group * 2 + hi) * BAND : (group * 2 + hi + 1) * BAND] for group in range(4)
        ]
        pair = pair_ref[hi : hi + 1, :]
        masked = jnp.concatenate(
            [jnp.where(pair == c, part, 0.0) for part in picked for c in range(PAIRS)], axis=0
        ).astype(BF16)
        sep = sep_ref[:, hi : hi + 1]
        column = jnp.where(
            sep >= NSEP // 2, sep - NSEP // 2, jnp.where(sep == 0, NSEP // 2, NSEP - sep)
        )
        onehot = jnp.where(
            column == lax.broadcasted_iota(jnp.int32, (flat, NSEP), 1), 1.0, 0.0
        ).astype(BF16)
        total = total + jnp.dot(masked, onehot, preferred_element_type=F32)
    for tile in range(NSEP // 128):
        grid_ref[tile] = total[:, tile * 128 : (tile + 1) * 128]

    flip = (
        lax.broadcasted_iota(jnp.int32, (HALF, HALF), 0)
        + lax.broadcasted_iota(jnp.int32, (HALF, HALF), 1)
        == HALF - 1
    )
    flip = jnp.where(flip, 1.0, 0.0).astype(BF16)
    odd_part = []
    edge = NSEP // 2 // FINE
    for f in range(BAND):
        cos_b = cos_ref[f, COARSE:, :]
        sin_b = sin_ref[f, COARSE:, :]
        for a in range(edge):
            cos_a = cos_ref[f, a : a + 1, :]
            sin_a = sin_ref[f, a : a + 1, :]
            at = pl.ds(a * FINE, FINE)
            table_buf[f, at, :HALF] = (cos_a * cos_b - sin_a * sin_b).astype(BF16)
            table_buf[f, at, HALF:] = (-(sin_a * cos_b + cos_a * sin_b)).astype(BF16)
        tiles = [grid_ref[tile, pl.ds(f, 2 * rows, stride=BAND), :] for tile in range(4)]
        cells = jnp.concatenate(
            [jnp.concatenate(tiles[:2], axis=1), jnp.concatenate(tiles[2:], axis=1)], axis=0
        ).astype(BF16)
        lone = tiles[2][:, :1]
        both = jnp.dot(cells, table_buf[f], preferred_element_type=F32)
        edge_cos = cos_ref[f, edge : edge + 1, :].astype(BF16).astype(F32)
        edge_sin = sin_ref[f, edge : edge + 1, :].astype(BF16).astype(F32)
        cos_part = both[:rows, :HALF] + both[2 * rows : 3 * rows, :HALF]
        cos_part = cos_part + lone[:rows] * (edge_cos - 1.0)
        sin_part = both[rows : 2 * rows, HALF:] - both[3 * rows :, HALF:]
        sin_part = sin_part + lone[rows:] * edge_sin
        even = cos_part + sin_part
        for r in range(RA_DEV):
            out_ref[f, r, :, :HALF] = even[r * PAIRS : (r + 1) * PAIRS]
        odd_part.append(cos_part - sin_part)
    rest = jnp.concatenate(odd_part, axis=0)
    turned = jnp.zeros(rest.shape, F32)
    for _ in range(3):
        piece = rest.astype(BF16)
        rest = rest - piece.astype(F32)
        turned = turned + jnp.dot(piece, flip, preferred_element_type=F32)
    for f in range(BAND):
        for r in range(RA_DEV):
            first = f * rows + r * PAIRS
            out_ref[f, r, :, HALF:] = turned[first : first + PAIRS]


def beam(block, pair_index, sep_index, angles):
    flat = BASES // 2
    pair = pair_index.reshape(N_BL, 2, BASE_LOC // 2).transpose(1, 0, 2).reshape(2, flat)
    sep = sep_index.reshape(N_BL, 2, BASE_LOC // 2).transpose(0, 2, 1).reshape(flat, 2)
    vmem = pl.BlockSpec(memory_space=pltpu.VMEM)
    return pl.pallas_call(
        beam_kernel,
        in_specs=[vmem] * 5,
        out_specs=vmem,
        out_shape=jax.ShapeDtypeStruct((BAND, RA_DEV, PAIRS, PIXELS), F32),
        scratch_shapes=[
            pltpu.VMEM((NSEP // 128, 2 * RA_DEV * PAIRS * BAND, 128), F32),
            pltpu.VMEM((BAND, NSEP // 2, 2 * HALF), BF16),
        ],
        compiler_params=pltpu.CompilerParams(vmem_limit_bytes=32 * MIB),
        name="beam",
    )(block, pair, sep, *angles)


def day_stage(visibility, day_weight, day_offset):
    visibility, day_weight = visibility[0], day_weight[0]
    other = lax.ppermute(select(day_offset, day_weight, visibility), "day", SWAP)
    return reduce_ring(chip_sums(day_offset, visibility, day_weight, other))


def beam_stage(summed, pair_index, sep_index):
    freq_at = (lax.axis_index("bl") * BAND + jnp.arange(BAND)).astype(F32)
    packed = pack(summed)
    pair_index, sep_index, freq_at, _ = lax.optimization_barrier(
        (pair_index, sep_index, freq_at, packed)
    )
    angles = base_angles(freq_at)
    block = lax.all_to_all(packed, "bl", split_axis=0, concat_axis=0, tiled=True)
    return beam(block, pair_index, sep_index, angles)


def local(visibility, day_weight, day_offset, pair_index, sep_index):
    summed = day_stage(visibility, day_weight, day_offset)
    return beam_stage(summed, pair_index, sep_index)


def solution(mesh):
    return jax.shard_map(
        local,
        mesh=mesh,
        in_specs=(P("day", None, None, "bl", None), P("day", "bl", None), P(), P(), P()),
        out_specs=P("bl", "day", None, None),
        check_vma=False,
    )
```

```python
import jax
import jax.numpy as jnp
from jax import lax
from jax.experimental import pallas as pl
from jax.experimental.pallas import tpu as pltpu
from jax.sharding import PartitionSpec as P

FREQ = 512
PAIRS = 4
NSEP = 512
PIXELS = 512
HALF = PIXELS // 2
RA = 32
RA_DEV = 2
SAMPLES = 16
DAYS = 16
BASES = 2048
N_BL = 32
BASE_LOC = BASES // N_BL
BAND = FREQ // N_BL
COARSE = 24
FINE = 16
CHIPS = 8
HELD = 8
SCALE = 128.0
SWAP = [(d, d ^ 1) for d in range(DAYS)]

F32 = jnp.float32
BF16 = jnp.bfloat16
F16 = jnp.float16
MIB = 1 << 20

phase_scale = 2.0 * 3.141592653589793 * 0.3048 / 299.792458


def bins_below(offset, core):
    return 2 * (offset >> 2) + jnp.clip((offset & 3) - 2 * core, 0, 2)


def select_kernel(offset_ref, weight_ref, vis_ref, out_ref, weight_buf, held_buf, sems):
    day = lax.axis_index("day")
    other = 1 - (day & 1)
    offset = offset_ref[day]
    first = bins_below(offset, other)
    load = pltpu.make_async_copy(weight_ref, weight_buf, sems.at[HELD])
    load.start()
    loads, stores = [], []
    for k in range(HELD):
        owned = first + k
        sample = 4 * (owned >> 1) + 2 * other + (owned & 1) - offset
        slot = owned & (HELD - 1)
        loads.append(pltpu.make_async_copy(vis_ref.at[sample], held_buf.at[k], sems.at[k]))
        loads[-1].start()
        stores.append(
            pltpu.make_async_copy(held_buf.at[k], out_ref.at[slot], sems.at[HELD + 1 + k])
        )
    load.wait()
    weight = weight_buf[...]
    high = weight.astype(BF16)
    held_buf[HELD, 0] = high
    held_buf[HELD, 1] = (weight - high.astype(F32)).astype(BF16)
    stores.append(
        pltpu.make_async_copy(held_buf.at[HELD], out_ref.at[HELD], sems.at[2 * HELD + 1])
    )
    stores[-1].start()
    for k in range(HELD):
        loads[k].wait()
        stores[k].start()
    for store in stores:
        store.wait()


def select(day_offset, day_weight, visibility):
    hbm = pl.BlockSpec(memory_space=pl.ANY)
    return pl.pallas_call(
        select_kernel,
        in_specs=[pl.BlockSpec(memory_space=pltpu.SMEM), hbm, hbm],
        out_specs=hbm,
        out_shape=jax.ShapeDtypeStruct((HELD + 1, 2, BASE_LOC, FREQ), BF16),
        scratch_shapes=[
            pltpu.VMEM((BASE_LOC, FREQ), F32),
            pltpu.VMEM((HELD + 1, 2, BASE_LOC, FREQ), BF16),
            pltpu.SemaphoreType.DMA((2 * HELD + 2,)),
        ],
        compiler_params=pltpu.CompilerParams(vmem_limit_bytes=60 * MIB),
        name="select",
    )(day_offset, day_weight, visibility)


SENDS = (
    ((3, 0), (3, 1), (1, 0), (1, 1)),
    ((5, 0), (5, 1), (7, 0), (7, 1)),
    ((4, 0),),
    ((4, 1),),
    ((2, 0), (2, 1)),
    ((6, 0), (6, 1)),
    ((0, 0), (0, 1)),
)


def chip_kernel(offset_ref, vis_ref, weight_ref, other_ref, *out_refs):
    day = lax.axis_index("day")
    core = day & 1
    chip = day >> 1
    offset = offset_ref[day]
    first = bins_below(offset_ref[day ^ 1], core)
    weight = weight_ref[...] * SCALE
    other_weight = (other_ref[HELD, 0].astype(F32) + other_ref[HELD, 1].astype(F32)) * SCALE
    for out_ref, bins in zip(out_refs, SENDS):
        for at, (distance, which) in enumerate(bins):
            owned = 2 * ((chip + distance) & (CHIPS - 1)) + which
            sample = 4 * (owned >> 1) + 2 * core + which - offset
            valid = jnp.logical_and(sample >= 0, sample < SAMPLES)
            held = jnp.logical_and(owned >= first, owned < first + HELD)
            sample = jnp.clip(sample, 0, SAMPLES - 1)
            own = weight * jnp.where(valid, 1.0, 0.0)
            other = other_weight * jnp.where(held, 1.0, 0.0)
            for x in range(2):
                out_ref[at, x] = (
                    vis_ref[sample, x].astype(F32) * own
                    + other_ref[owned & (HELD - 1), x].astype(F32) * other
                )


def chip_sums(day_offset, visibility, day_weight, other):
    rows = 16
    block = lambda count: pl.BlockSpec((count, 2, rows, FREQ), lambda i: (0, 0, i, 0))
    return pl.pallas_call(
        chip_kernel,
        grid=(BASE_LOC // rows,),
        in_specs=[
            pl.BlockSpec(memory_space=pltpu.SMEM),
            block(SAMPLES),
            pl.BlockSpec((rows, FREQ), lambda i: (i, 0)),
            block(HELD + 1),
        ],
        out_specs=[block(len(bins)) for bins in SENDS],
        out_shape=[
            (pltpu.HBM if at >= 4 else jax.ShapeDtypeStruct)((len(bins), 2, BASE_LOC, FREQ), F32)
            for at, bins in enumerate(SENDS)
        ],
        compiler_params=pltpu.CompilerParams(vmem_limit_bytes=16 * MIB),
        name="chip_sums",
    )(day_offset, visibility, day_weight, other)


def send(values, distance):
    pairs = [
        (2 * y + c, 2 * ((y + distance) % CHIPS) + c) for y in range(CHIPS) for c in range(2)
    ]
    return lax.ppermute(values, "day", pairs)


def reduce_ring(sums, late):
    first = lax.optimization_barrier([part.astype(F16) for part in sums[:4]])
    near_up, near_down = send(first[0], 1), send(first[1], -1)
    far_up, far_down = send(first[2], 2), send(first[3], -2)
    middle_up = sums[4] + near_up[:2].astype(F32)
    middle_up = middle_up + jnp.pad(far_up.astype(F32), ((0, 1), (0, 0), (0, 0), (0, 0)))
    middle_down = sums[5] + near_down[:2].astype(F32)
    middle_down = middle_down + jnp.pad(far_down.astype(F32), ((1, 0), (0, 0), (0, 0), (0, 0)))
    middle_up, middle_down = middle_up.astype(F16), middle_down.astype(F16)
    last_up, last_down = send(middle_up, 2), send(middle_down, -2)
    late = lax.optimization_barrier((late, last_up))[0]
    summed = (
        sums[6]
        + near_up[2:].astype(F32)
        + near_down[2:].astype(F32)
        + last_up.astype(F32)
        + last_down.astype(F32)
    )
    return summed, late


def gather_weights(day_weight):
    same = [[2 * y + c for y in range(CHIPS)] for c in range(2)]
    copies = jnp.broadcast_to(day_weight.astype(F16)[None], (CHIPS, BASE_LOC, FREQ))
    return lax.all_to_all(
        copies, "day", split_axis=0, concat_axis=0, axis_index_groups=same, tiled=True
    )


def inverse_total(day_offset, weights):
    day = lax.axis_index("day")
    offsets = jnp.where((day & 1) == 0, day_offset[0::2], day_offset[1::2])
    at = jnp.arange(2 * RA_DEV)
    bins = (day ^ (at // RA_DEV)) * RA_DEV + at % RA_DEV
    sample = bins[:, None] - offsets[None, :]
    valid = jnp.logical_and(sample >= 0, sample < SAMPLES).astype(F32)
    totals = jnp.sum(valid[:, :, None, None] * weights[None].astype(F32), axis=1)
    other = lax.ppermute(totals[RA_DEV:], "day", SWAP)
    return (1.0 / SCALE) / (totals[:RA_DEV] + other)


def base_angles(freq_at):
    factor = phase_scale * (800.0 - 400.0 * (freq_at + 0.5) / FREQ)
    sine_dir = -1.0 + 2.0 * (jnp.arange(HALF).astype(F32) + 0.5) / PIXELS
    separation = jnp.concatenate([jnp.arange(COARSE) * FINE, jnp.arange(FINE)]).astype(F32)
    phase = factor[:, None, None] * separation[None, :, None] * sine_dir[None, None, :]
    return jnp.cos(phase), jnp.sin(phase)


def pack_blocks(pieces, out_ref, rows):
    lane_group = lax.broadcasted_iota(jnp.int32, (8, 128), 1) // BAND
    for tile in range(FREQ // 128):
        parts = [piece[:, tile * 128 : (tile + 1) * 128] for piece in pieces]
        for step in (4, 2, 1):
            keep = (lane_group & step) == 0
            mixed = list(parts)
            for low in range(8):
                if low & step:
                    continue
                high = low | step
                mixed[low] = jnp.where(keep, parts[low], pltpu.roll(parts[high], step * BAND, 1))
                mixed[high] = jnp.where(
                    keep, pltpu.roll(parts[low], 128 - step * BAND, 1), parts[high]
                )
            parts = mixed
        for group in range(8):
            out_ref[tile * 8 + group, rows, :] = parts[group].astype(BF16)


def pack_kernel(sum_ref, inverse_ref, out_ref):
    half = BASE_LOC // 2
    for first in range(0, half, 16):
        for sub in range(0, 16, 8):
            rows = pl.ds(first + sub, 8)
            pieces = []
            for x in range(2):
                for r in range(RA_DEV):
                    for hi in range(2):
                        rows_in = pl.ds(hi * half + first + sub, 8)
                        pieces.append(
                            sum_ref[r, x, rows_in, :] * inverse_ref[r, rows_in, :]
                        )
            pack_blocks(pieces, out_ref, rows)


def pack(summed, inverse):
    vmem = pl.BlockSpec(memory_space=pltpu.VMEM)
    return pl.pallas_call(
        pack_kernel,
        in_specs=[vmem, vmem],
        out_specs=vmem,
        out_shape=jax.ShapeDtypeStruct((N_BL, BASE_LOC // 2, 128), BF16),
        compiler_params=pltpu.CompilerParams(vmem_limit_bytes=16 * MIB),
        name="pack",
    )(summed, inverse)


def beam_kernel(block_ref, pair_ref, sep_ref, cos_ref, sin_ref, out_ref, grid_ref, table_buf):
    flat = BASES // 2
    rows = RA_DEV * PAIRS

    turned = block_ref[...].astype(F32).reshape(flat, 128).T
    total = jnp.zeros((2 * rows * BAND, NSEP), F32)
    for hi in range(2):
        picked = [
            turned[(group * 2 + hi) * BAND : (group * 2 + hi + 1) * BAND] for group in range(4)
        ]
        pair = pair_ref[hi : hi + 1, :]
        masked = jnp.concatenate(
            [jnp.where(pair == c, part, 0.0) for part in picked for c in range(PAIRS)], axis=0
        ).astype(BF16)
        sep = sep_ref[:, hi : hi + 1]
        column = jnp.where(
            sep >= NSEP // 2, sep - NSEP // 2, jnp.where(sep == 0, NSEP // 2, NSEP - sep)
        )
        onehot = jnp.where(
            column == lax.broadcasted_iota(jnp.int32, (flat, NSEP), 1), 1.0, 0.0
        ).astype(BF16)
        total = total + jnp.dot(masked, onehot, preferred_element_type=F32)
    for tile in range(NSEP // 128):
        grid_ref[tile] = total[:, tile * 128 : (tile + 1) * 128]

    flip = (
        lax.broadcasted_iota(jnp.int32, (HALF, HALF), 0)
        + lax.broadcasted_iota(jnp.int32, (HALF, HALF), 1)
        == HALF - 1
    )
    flip = jnp.where(flip, 1.0, 0.0).astype(BF16)
    odd_part = []
    edge = NSEP // 2 // FINE
    for f in range(BAND):
        cos_b = cos_ref[f, COARSE:, :]
        sin_b = sin_ref[f, COARSE:, :]
        for a in range(edge):
            cos_a = cos_ref[f, a : a + 1, :]
            sin_a = sin_ref[f, a : a + 1, :]
            at = pl.ds(a * FINE, FINE)
            table_buf[f, at, :HALF] = (cos_a * cos_b - sin_a * sin_b).astype(BF16)
            table_buf[f, at, HALF:] = (-(sin_a * cos_b + cos_a * sin_b)).astype(BF16)
        tiles = [grid_ref[tile, pl.ds(f, 2 * rows, stride=BAND), :] for tile in range(4)]
        cells = jnp.concatenate(
            [jnp.concatenate(tiles[:2], axis=1), jnp.concatenate(tiles[2:], axis=1)], axis=0
        ).astype(BF16)
        lone = tiles[2][:, :1]
        both = jnp.dot(cells, table_buf[f], preferred_element_type=F32)
        edge_cos = cos_ref[f, edge : edge + 1, :].astype(BF16).astype(F32)
        edge_sin = sin_ref[f, edge : edge + 1, :].astype(BF16).astype(F32)
        cos_part = both[:rows, :HALF] + both[2 * rows : 3 * rows, :HALF]
        cos_part = cos_part + lone[:rows] * (edge_cos - 1.0)
        sin_part = both[rows : 2 * rows, HALF:] - both[3 * rows :, HALF:]
        sin_part = sin_part + lone[rows:] * edge_sin
        even = cos_part + sin_part
        for r in range(RA_DEV):
            out_ref[f, r, :, :HALF] = even[r * PAIRS : (r + 1) * PAIRS]
        odd_part.append(cos_part - sin_part)
    rest = jnp.concatenate(odd_part, axis=0)
    turned = jnp.zeros(rest.shape, F32)
    for _ in range(3):
        piece = rest.astype(BF16)
        rest = rest - piece.astype(F32)
        turned = turned + jnp.dot(piece, flip, preferred_element_type=F32)
    for f in range(BAND):
        for r in range(RA_DEV):
            first = f * rows + r * PAIRS
            out_ref[f, r, :, HALF:] = turned[first : first + PAIRS]


def beam(block, pair_index, sep_index, angles):
    flat = BASES // 2
    pair = pair_index.reshape(N_BL, 2, BASE_LOC // 2).transpose(1, 0, 2).reshape(2, flat)
    sep = sep_index.reshape(N_BL, 2, BASE_LOC // 2).transpose(0, 2, 1).reshape(flat, 2)
    vmem = pl.BlockSpec(memory_space=pltpu.VMEM)
    return pl.pallas_call(
        beam_kernel,
        in_specs=[vmem] * 5,
        out_specs=vmem,
        out_shape=jax.ShapeDtypeStruct((BAND, RA_DEV, PAIRS, PIXELS), F32),
        scratch_shapes=[
            pltpu.VMEM((NSEP // 128, 2 * RA_DEV * PAIRS * BAND, 128), F32),
            pltpu.VMEM((BAND, NSEP // 2, 2 * HALF), BF16),
        ],
        compiler_params=pltpu.CompilerParams(vmem_limit_bytes=32 * MIB),
        name="beam",
    )(block, pair, sep, *angles)


def day_stage(visibility, day_weight, day_offset):
    visibility, day_weight = visibility[0], day_weight[0]
    other = lax.ppermute(select(day_offset, day_weight, visibility), "day", SWAP)
    weights = gather_weights(day_weight)
    sums = chip_sums(day_offset, visibility, day_weight, other)
    summed, weights = reduce_ring(sums, weights)
    return summed, inverse_total(day_offset, weights)


def beam_stage(summed, inverse, pair_index, sep_index):
    freq_at = (lax.axis_index("bl") * BAND + jnp.arange(BAND)).astype(F32)
    packed = pack(summed, inverse)
    pair_index, sep_index, freq_at, _ = lax.optimization_barrier(
        (pair_index, sep_index, freq_at, packed)
    )
    angles = base_angles(freq_at)
    block = lax.all_to_all(packed, "bl", split_axis=0, concat_axis=0, tiled=True)
    return beam(block, pair_index, sep_index, angles)


def local(visibility, day_weight, day_offset, pair_index, sep_index):
    summed, inverse = day_stage(visibility, day_weight, day_offset)
    return beam_stage(summed, inverse, pair_index, sep_index)


def solution(mesh):
    return jax.shard_map(
        local,
        mesh=mesh,
        in_specs=(P("day", None, None, "bl", None), P("day", "bl", None), P(), P(), P()),
        out_specs=P("bl", "day", None, None),
        check_vma=False,
    )
```
